256 devices in a mesh: rows: 16 (over z, core), cols: 16 (over y, x).
Axes of the slice: x: 4, y: 4, z: 8, core: 2. Of those that a mesh axis runs over, the one named last changes fastest.
Arguments:
- values: float32 [131072, 128], P(('rows', 'cols')), may hold values from -196608 to 196608
- tile_users: int32 [131072, 128], P(('rows', 'cols')), may hold values from 0 to 8191
- tile_items: int32 [131072], P(('rows', 'cols')), may hold values from 0 to 4095
- tile_words: int32 [131072], P(('rows', 'cols')), may hold values from 0 to 4095
- tile_count: int32 [256], P(('rows', 'cols')), may hold values from 128 to 512, as said below
- factor_items: bfloat16 [65536, 128], P(('rows', 'cols'))
- factor_words: bfloat16 [65536, 128], P(('rows', 'cols'))
Outputs:
- factor_users: float32 [131072, 128], P(('rows', 'cols'))
The draws below stay inside these ranges and needn't reach their ends.
Inputs may be any that keep to these rules, and one draw needn't show every extreme that they name: `tile_count`: 512 is reached on some device in every draw.
All inputs are finite; a program needn't handle non-finite values.
Results may differ from the reference program's by a relative error of at most 0.0003.
Values may be sent and summed in bfloat16 or wider, within the bound.
No kernel may reach another device: no remote copies, remote signals or barrier semaphores. Data moves between devices by JAX's collectives and lax.ppermute only.
A program may use at most 64 MiB of HBM per device.

```python
import math
import jax
import jax.numpy as jnp
from jax import lax

RANK = 128
FIBER = 128
TILE_CAP = 512
I_DEV = 512
J_DEV = 256
K_DEV = 256
ITEMS = 65536
WORDS = 65536
TILES = 131072
N_ROWS = 16
N_COLS = 16


def shape_factor(key, mixed_base, mixing, per_device):
    total = mixed_base.shape[0]
    jitter_key, column_key = jax.random.split(key)
    mixed = mixed_base + mixing * jnp.roll(mixed_base, 1, axis=1)
    index_rows = jnp.arange(total)
    device = index_rows // per_device
    row_group = (device // N_COLS).astype(jnp.float32)
    col_group = (device % N_COLS).astype(jnp.float32)
    rise = 1.0 + (row_group / max(N_ROWS - 1, 1) + col_group / max(N_COLS - 1, 1))
    jitter = jnp.exp(math.log(4.0) * (jax.random.uniform(jitter_key, (total,), jnp.float32) - 0.5))
    columns = jnp.exp(math.log(3.0) * jax.random.uniform(column_key, (RANK,), jnp.float32))
    scaled = mixed * (rise * jitter)[:, None] * columns[None, :] / math.sqrt(6.0 * total)
    return scaled.astype(jnp.bfloat16)


def draw_factor_items(key, part):
    key = jax.random.fold_in(key, 11)
    base_key, shape_key = jax.random.split(key)
    mixed_base = jax.random.normal(base_key, (ITEMS, RANK), jnp.float32)
    return shape_factor(shape_key, mixed_base, 0.5, J_DEV)


def draw_factor_words(key, part):
    key = jax.random.fold_in(key, 23)
    base_key, shape_key = jax.random.split(key)
    mixed_base = jax.random.normal(base_key, (WORDS, RANK), jnp.float32)
    return shape_factor(shape_key, mixed_base, 0.5, K_DEV)


def draw_tile_count(key, part):
    key = jax.random.fold_in(key, 37)
    heavy_key, light_key, full_key, peak_key = jax.random.split(key, 4)
    device_total = N_ROWS * N_COLS
    device = jnp.arange(device_total, dtype=jnp.int32)
    heavy = jax.random.randint(heavy_key, (), 0, N_ROWS, dtype=jnp.int32)
    light = TILE_CAP // 4 + jax.random.randint(light_key, (device_total,), 0, TILE_CAP // 4 + 1, dtype=jnp.int32)
    nearly = TILE_CAP - jax.random.randint(full_key, (device_total,), 0, TILE_CAP // 8 + 1, dtype=jnp.int32)
    counts = jnp.where(device // N_COLS == heavy, nearly, light)
    peak = heavy * N_COLS + jax.random.randint(peak_key, (), 0, N_COLS, dtype=jnp.int32)
    counts = jnp.where(device == peak, TILE_CAP, counts)
    return counts.astype(jnp.int32)


def plant(values, stream_key, least, top_value):
    shape = values.shape
    spot = [jax.random.randint(jax.random.fold_in(stream_key, axis), (), 0, shape[axis]) for axis in range(len(shape))]
    values = values.at[tuple(spot)].set(least)
    longest = shape.index(max(shape))
    spot[longest] = (spot[longest] + 1) % shape[longest]
    return values.at[tuple(spot)].set(top_value)


def block_levels(own_key, shape, shards, least, top_value):
    loudness = 1.0
    for dim, shards_of in shards:
        draws = jax.random.uniform(jax.random.fold_in(jax.random.fold_in(own_key, 6), dim), (shards_of,), jnp.float32, least / len(shards), top_value / len(shards))
        loudness = loudness * jnp.repeat(jnp.exp(draws), shape[dim] // shards_of).reshape((-1,) + (1,) * (len(shape) - 1 - dim))
    return loudness


def centred(rng, dims, deviation, most, shards=(), held_as=jnp.bfloat16):
    drawn = deviation * jax.random.normal(rng, dims, jnp.float32)
    if shards:
        drawn = drawn * block_levels(rng, dims, shards, -0.22, 0.18)
    return jnp.clip(drawn, -most, most).astype(held_as)


def setup_inputs(seed: int = 0) -> dict:
    key_of = jax.random.split(jax.random.key(seed), 8)
    return {
        "values": centred(key_of[0], (TILES, FIBER), (J_DEV * N_ROWS * N_COLS // 2), 196608.0, ((0, 256),), jnp.float32),
        "tile_users": plant(jax.random.randint(key_of[1], (TILES, FIBER), 0, I_DEV * N_COLS), jax.random.fold_in(key_of[1], 1), 0, (I_DEV * N_COLS) - 1).astype(jnp.int32),
        "tile_items": plant(jax.random.randint(key_of[2], (TILES,), 0, J_DEV * N_ROWS), jax.random.fold_in(key_of[2], 1), 0, (J_DEV * N_ROWS) - 1).astype(jnp.int32),
        "tile_words": plant(jax.random.randint(key_of[3], (TILES,), 0, K_DEV * N_ROWS), jax.random.fold_in(key_of[3], 1), 0, (K_DEV * N_ROWS) - 1).astype(jnp.int32),
        "tile_count": draw_tile_count(jax.random.fold_in(key_of[7], 71), 0),
        "factor_items": draw_factor_items(jax.random.fold_in(key_of[7], 71), 0),
        "factor_words": draw_factor_words(jax.random.fold_in(key_of[7], 71), 0),
    }


def self_product(matrix):
    return lax.dot_general(matrix.astype(jnp.float32), matrix.astype(jnp.float32), (((0,), (0,)), ((), ())), preferred_element_type=jnp.float32)

def reference(values, tile_users, tile_items, tile_words, tile_count, factor_items, factor_words):
    device_total = N_ROWS * N_COLS
    item_rows = factor_items.astype(jnp.float32)
    word_rows = factor_words.astype(jnp.float32)
    gram = self_product(factor_items) * self_product(factor_words)

    def device_term(partial_value, device):
        row_group = device // N_COLS
        col_group = device % N_COLS
        offset = device * TILE_CAP
        slot_values = lax.dynamic_slice_in_dim(values, offset, TILE_CAP, 0)
        slot_users = lax.dynamic_slice_in_dim(tile_users, offset, TILE_CAP, 0)
        item_local = lax.dynamic_slice_in_dim(tile_items, offset, TILE_CAP, 0)
        word_local = lax.dynamic_slice_in_dim(tile_words, offset, TILE_CAP, 0)
        item_global = (item_local // J_DEV * N_COLS + col_group) * J_DEV + item_local % J_DEV
        word_global = (word_local // K_DEV * N_COLS + col_group) * K_DEV + word_local % K_DEV
        khatri = item_rows[item_global] * word_rows[word_global]
        live_mask = jnp.arange(TILE_CAP, dtype=jnp.int32) < tile_count[device]
        weights = jnp.where(live_mask[:, None], slot_values, jnp.zeros_like(slot_values))
        terms = (weights[:, :, None] * khatri[:, None, :]).reshape(-1, RANK)
        targets = (row_group * I_DEV * N_COLS + slot_users).reshape(-1)
        return (partial_value.at[targets].add(terms), None)
    start_rows = jnp.zeros((I_DEV * device_total, RANK), jnp.float32)
    mttkrp, _ = lax.scan(device_term, start_rows, jnp.arange(device_total, dtype=jnp.int32))
    lower = jnp.linalg.cholesky(gram)
    return jax.scipy.linalg.cho_solve((lower, True), mttkrp.T).T
```

```python
import functools

import jax
import jax.numpy as jnp
from jax import lax
from jax.experimental import pallas as pl
from jax.experimental.pallas import tpu as pltpu
from jax.sharding import PartitionSpec as P

RANK = 128
FIBER = 128
TILES = 512
ROWS = 256
OWN = 512
PEERS = 16
USERS = OWN * PEERS
LO = 128
HI = USERS // LO
EXTRA = 16
STEP = 128.0
TOP = 32767.0
NT = (((1,), (1,)), ((), ()))
TN = (((0,), (0,)), ((), ()))
MIB = 1024 * 1024


def build_body(v_ref, u_ref, high_ref, low_ref, acc_ref, *, block, group):
    hi_iota = lax.broadcasted_iota(jnp.int32, (HI, FIBER), 0)
    lo_iota = lax.broadcasted_iota(jnp.int32, (LO, FIBER), 0)

    def add_group(g, carry):
        for k in range(group):
            t = g * group + k
            v = v_ref[pl.ds(t, 1), :]
            u = u_ref[pl.ds(t, 1), :]
            vh = v.astype(jnp.bfloat16).astype(jnp.float32)
            vl = v - vh
            hit = hi_iota == (u >> 7)
            left = jnp.concatenate(
                [jnp.where(hit, vh, 0.0).astype(jnp.bfloat16), jnp.where(hit, vl, 0.0).astype(jnp.bfloat16)], axis=1
            )
            one = jnp.where(lo_iota == (u & 127), 1.0, 0.0).astype(jnp.bfloat16)
            right = jnp.concatenate([one, one], axis=1)
            acc_ref[pl.ds(t, HI, stride=block), :] = lax.dot_general(
                left, right, NT, preferred_element_type=jnp.float32
            )
        return carry

    lax.fori_loop(0, block // group, add_group, 0)
    weight = acc_ref[...].reshape(HI, block, LO)
    high = weight.astype(jnp.bfloat16)
    high_ref[...] = high
    low_ref[...] = (weight - high.astype(jnp.float32)).astype(jnp.bfloat16)


def build_weights(values, users, block=32, group=8, interpret=False):
    return pl.pallas_call(
        functools.partial(build_body, block=block, group=group),
        grid=(TILES // block,),
        in_specs=[pl.BlockSpec((block, FIBER), lambda i: (i, 0))] * 2,
        out_specs=[pl.BlockSpec((HI, block, LO), lambda i: (0, i, 0))] * 2,
        out_shape=[jax.ShapeDtypeStruct((HI, TILES, LO), jnp.bfloat16)] * 2,
        scratch_shapes=[pltpu.VMEM((HI * block, LO), jnp.float32)],
        compiler_params=pltpu.CompilerParams(vmem_limit_bytes=40 * MIB),
        name="build_weights",
        interpret=interpret,
    )(values, users)


def product_body(item_at, word_at, count, source, *refs, n_pieces, per_step):
    pieces = refs[: 2 * n_pieces]
    high_ref, low_ref, out_ref, item_ref, word_ref, khatri_ref, parts_ref = refs[2 * n_pieces :]

    @pl.when(pl.program_id(0) == 0)
    def _():
        for i in range(n_pieces):
            at = pl.multiple_of(source[i] * ROWS, ROWS)
            item_ref[pl.ds(at, ROWS), :] = pieces[i][...].astype(jnp.float32)
            word_ref[pl.ds(at, ROWS), :] = pieces[n_pieces + i][...].astype(jnp.float32)

        def take(g, carry):
            for k in range(8):
                t = g * 8 + k
                khatri_ref[pl.ds(t, 1), :] = item_ref[pl.ds(item_at[t], 1), :] * word_ref[pl.ds(word_at[t], 1), :]
            return carry

        lax.fori_loop(0, TILES // 8, take, 0)
        live = lax.broadcasted_iota(jnp.int32, (TILES, RANK), 0) < count[0]
        khatri = jnp.where(live, khatri_ref[...], 0.0).T
        high = khatri.astype(jnp.bfloat16)
        parts_ref[:RANK, :] = high
        parts_ref[RANK:, :] = (khatri - high.astype(jnp.float32)).astype(jnp.bfloat16)

    high = jnp.concatenate([high_ref[i] for i in range(per_step)], axis=1)
    low = jnp.concatenate([low_ref[i] for i in range(per_step)], axis=1)
    both = jnp.dot(parts_ref[...], high, preferred_element_type=jnp.float32)
    rest = jnp.dot(parts_ref[:RANK, :], low, preferred_element_type=jnp.float32)
    total = both[:RANK] + (both[RANK:] + rest)
    most = jnp.max(jnp.abs(total), axis=1, keepdims=True)
    level = jnp.ceil(jnp.log2(jnp.maximum(most, 1e-35)) * STEP + 1.0)
    coded = jnp.round(total * jnp.exp2(level * (-1.0 / STEP)) * TOP)
    out_ref[0, :RANK, :] = coded.astype(jnp.int32).astype(jnp.int16)
    level_row = jnp.broadcast_to(level, (RANK, RANK)).T[:EXTRA]
    out_ref[0, RANK:, :] = jnp.tile(level_row, (1, OWN // RANK)).astype(jnp.int32).astype(jnp.int16)


def products(item_at, word_at, count, source, items, words, high, low, interpret=False):
    n = len(items)
    per_step = OWN // LO
    whole = [pl.BlockSpec(x.shape, lambda i, *_: (0, 0)) for x in (*items, *words)]
    return pl.pallas_call(
        functools.partial(product_body, n_pieces=n, per_step=per_step),
        grid_spec=pltpu.PrefetchScalarGridSpec(
            num_scalar_prefetch=4,
            grid=(PEERS,),
            in_specs=whole + [pl.BlockSpec((per_step, TILES, LO), lambda i, *_: (i, 0, 0))] * 2,
            out_specs=pl.BlockSpec((1, RANK + EXTRA, OWN), lambda i, *_: (i, 0, 0)),
            scratch_shapes=[
                pltpu.VMEM((PEERS * ROWS, RANK), jnp.float32),
                pltpu.VMEM((PEERS * ROWS, RANK), jnp.float32),
                pltpu.VMEM((TILES, RANK), jnp.float32),
                pltpu.VMEM((2 * RANK, TILES), jnp.bfloat16),
            ],
        ),
        out_shape=jax.ShapeDtypeStruct((PEERS, RANK + EXTRA, OWN), jnp.int16),
        compiler_params=pltpu.CompilerParams(vmem_limit_bytes=40 * MIB),
        name="products",
        interpret=interpret,
    )(item_at, word_at, count, source, *items, *words, high, low)


def finish_body(coded_ref, inverse_ref, out_ref, sum_ref):
    step = pl.program_id(0)

    @pl.when(step == 0)
    def _():
        sum_ref[...] = jnp.zeros_like(sum_ref)

    levels = coded_ref[0, RANK:, :RANK].astype(jnp.int32).astype(jnp.float32)
    level = jnp.broadcast_to(levels[:1], (RANK, RANK)).T[:, :1]
    scale = jnp.exp2(level * (1.0 / STEP)) * (1.0 / TOP)
    sum_ref[...] += coded_ref[0, :RANK, :].astype(jnp.int32).astype(jnp.float32) * scale

    @pl.when(step == pl.num_programs(0) - 1)
    def _():
        out_ref[...] = lax.dot_general(
            sum_ref[...], inverse_ref[...], TN, precision=lax.Precision.HIGHEST, preferred_element_type=jnp.float32
        )


def finish(coded, inverse, interpret=False):
    return pl.pallas_call(
        finish_body,
        grid=(PEERS,),
        in_specs=[
            pl.BlockSpec((1, RANK + EXTRA, OWN), lambda i: (i, 0, 0)),
            pl.BlockSpec((RANK, RANK), lambda i: (0, 0)),
        ],
        out_specs=pl.BlockSpec((OWN, RANK), lambda i: (0, 0)),
        out_shape=jax.ShapeDtypeStruct((OWN, RANK), jnp.float32),
        scratch_shapes=[pltpu.VMEM((RANK, OWN), jnp.float32)],
        compiler_params=pltpu.CompilerParams(vmem_limit_bytes=40 * MIB),
        name="finish",
        interpret=interpret,
    )(coded, inverse)


def gram_body(item_ref, word_ref, out_ref):
    for i, ref in enumerate((item_ref, word_ref)):
        x = ref[...]
        g = lax.dot_general(x, x, TN, preferred_element_type=jnp.float32)
        out_ref[:, i] = g.reshape(PEERS, RANK // PEERS, RANK)


def local_grams(items, words, interpret=False):
    return pl.pallas_call(
        gram_body,
        out_shape=jax.ShapeDtypeStruct((PEERS, 2, RANK // PEERS, RANK), jnp.float32),
        name="local_grams",
        interpret=interpret,
    )(items, words)


def gathered(x):
    def moved(by):
        return [(2 * z + c, 2 * ((z + by) % 8) + c) for z in range(8) for c in range(2)]

    across = [(i, i ^ 1) for i in range(PEERS)]
    ahead = behind = x
    found = [(x, 0)]
    for k in range(1, 5):
        ahead = lax.ppermute(ahead, "rows", moved(1))
        found.append((ahead, -2 * k))
        if k < 4:
            behind = lax.ppermute(behind, "rows", moved(-1))
            found.append((behind, 2 * k))
    me = lax.axis_index("rows")
    z2, c = me // 2 * 2, me % 2
    here = [((z2 + by) % PEERS) for _, by in found]
    source = jnp.stack([p + c for p in here] + [p + 1 - c for p in here])
    pieces = [p for p, _ in found] + [lax.ppermute(p, "rows", across) for p, _ in found]
    return pieces, source


def gram_inverse(items, words):
    mine = lax.all_to_all(local_grams(items, words), "cols", 0, 0).sum(0)
    mine = lax.all_to_all(jnp.broadcast_to(mine[None], (PEERS, *mine.shape)), "rows", 0, 0).sum(0)
    part = mine[0] * mine[1]
    gram = lax.all_to_all(jnp.broadcast_to(part[None], (PEERS, *part.shape)), "cols", 0, 0).reshape(RANK, RANK)
    lower = jnp.linalg.cholesky(gram)
    return jax.scipy.linalg.cho_solve((lower, True), jnp.eye(RANK, dtype=jnp.float32))


def on_device(values, tile_users, tile_items, tile_words, tile_count, factor_items, factor_words):
    items, source = gathered(factor_items)
    words, _ = gathered(factor_words)
    high, low = build_weights(values, tile_users)
    inverse = gram_inverse(factor_items, factor_words)
    coded = products(tile_items, tile_words, tile_count, source, items, words, high, low)
    coded = lax.all_to_all(coded, "cols", 0, 0)
    return finish(coded, inverse)


def solution(mesh):
    placed = (
        P(("rows", "cols"), None),
        P(("rows", "cols"), None),
        P(("rows", "cols")),
        P(("rows", "cols")),
        P(("rows", "cols")),
        P(("rows", "cols"), None),
        P(("rows", "cols"), None),
    )
    return jax.shard_map(
        on_device, mesh=mesh, in_specs=placed, out_specs=P(("rows", "cols"), None), check_vma=False
    )
```

```python
import functools

import jax
import jax.numpy as jnp
from jax import lax
from jax.experimental import pallas as pl
from jax.experimental.pallas import tpu as pltpu
from jax.sharding import PartitionSpec as P

RANK = 128
FIBER = 128
TILES = 512
ROWS = 256
OWN = 512
PEERS = 16
USERS = OWN * PEERS
LO = 128
HI = USERS // LO
EXTRA = 16
PARTS = 4
SLICES = 4
PIVOTS = 4
SLICE = RANK // SLICES
FOLD = 4
PART = TILES // PARTS
STEP = 128.0
TOP = 32767.0
NT = (((1,), (1,)), ((), ()))
TN = (((0,), (0,)), ((), ()))
MIB = 1024 * 1024


def in_hbm(shape, dtype, interpret):
    return jax.ShapeDtypeStruct(shape, dtype) if interpret else pltpu.HBM(shape, dtype)


def build_body(v_ref, u_ref, after_ref, high_ref, low_ref, acc_ref, *, block):
    del after_ref
    pitch = block + 1
    hi_iota = lax.broadcasted_iota(jnp.int32, (HI, FIBER), 0)
    lo_iota = lax.broadcasted_iota(jnp.int32, (LO, FIBER), 0)

    def add_block(g, carry):
        at = pl.multiple_of(g * block, block)
        for k in range(block):
            v = v_ref[pl.ds(at + k, 1), :]
            u = u_ref[pl.ds(at + k, 1), :]
            vh = v.astype(jnp.bfloat16).astype(jnp.float32)
            vl = v - vh
            hit = hi_iota == (u >> 7)
            left = jnp.concatenate(
                [jnp.where(hit, vh, 0.0).astype(jnp.bfloat16), jnp.where(hit, vl, 0.0).astype(jnp.bfloat16)], axis=1
            )
            one = jnp.where(lo_iota == (u & 127), 1.0, 0.0).astype(jnp.bfloat16)
            right = jnp.concatenate([one, one], axis=1)
            acc_ref[pl.ds(k, HI, stride=pitch), :] = lax.dot_general(
                left, right, NT, preferred_element_type=jnp.float32
            )
        for h in range(HI):
            weight = acc_ref[pl.ds(h * pitch, block), :]
            high = weight.astype(jnp.bfloat16)
            high_ref[h, pl.ds(at, block), :] = high
            low_ref[h, pl.ds(at, block), :] = (weight - high.astype(jnp.float32)).astype(jnp.bfloat16)
        return carry

    lax.fori_loop(0, PART // block, add_block, 0)


def build_weights(values, users, part, after, block=32, interpret=False):
    return pl.pallas_call(
        functools.partial(build_body, block=block),
        grid=(1,),
        in_specs=[pl.BlockSpec((PART, FIBER), lambda i: (part, 0))] * 2 + [pl.BlockSpec(memory_space=pl.ANY)],
        out_specs=[pl.BlockSpec(memory_space=pltpu.VMEM)] * 2,
        out_shape=[pltpu.VMEM((HI, PART, LO), jnp.bfloat16)] * 2 if not interpret else [jax.ShapeDtypeStruct((HI, PART, LO), jnp.bfloat16)] * 2,
        scratch_shapes=[pltpu.VMEM((HI * (block + 1), LO), jnp.float32)],
        compiler_params=pltpu.CompilerParams(vmem_limit_bytes=20 * MIB),
        cost_estimate=pl.CostEstimate(flops=6 * 10**9, bytes_accessed=20 * 10**6, transcendentals=0),
        name="build_weights",
        interpret=interpret,
    )(values, users, after)


def sources(me):
    z, c = me // 2, me % 2
    way = 1 - 2 * c
    blocks = [(z, c), (z, 1 - c)]
    for k in range(1, 4):
        blocks += [(z - k * way, c), (z - k * way, 1 - c)]
    blocks.append((z - 4 * way, c))
    for k in range(1, 4):
        blocks += [(z + k * way, 1 - c), (z + k * way, c)]
    blocks.append((z + 4 * way, 1 - c))
    return [(chip + 8) % 8 * 2 + core for chip, core in blocks]


def product_body(item_at, word_at, count, *refs, sizes, per_step, me):
    pieces = refs[: len(sizes)]
    weights = refs[len(sizes) : len(sizes) + 2 * PARTS]
    out_ref, item_ref, word_ref, khatri_ref, parts_ref = refs[len(sizes) + 2 * PARTS :]

    @pl.when(pl.program_id(0) == 0)
    def _():
        source = iter(sources(lax.axis_index("rows") if me is None else me))
        for ref, size in zip(pieces, sizes, strict=True):
            for j in range(size):
                at = pl.multiple_of(next(source) * ROWS, ROWS)
                item_ref[pl.ds(at, ROWS), :] = ref[2 * j * ROWS : (2 * j + 1) * ROWS, :].astype(jnp.float32)
                word_ref[pl.ds(at, ROWS), :] = ref[(2 * j + 1) * ROWS : (2 * j + 2) * ROWS, :].astype(jnp.float32)

        def take(g, carry):
            for k in range(16):
                t = g * 16 + k
                khatri_ref[pl.ds(t, 1), :] = item_ref[pl.ds(item_at[t], 1), :] * word_ref[pl.ds(word_at[t], 1), :]
            return carry

        lax.fori_loop(0, TILES // 16, take, 0)
        live = lax.broadcasted_iota(jnp.int32, (TILES, RANK), 0) < count[0]
        khatri = jnp.where(live, khatri_ref[...], 0.0).T
        high = khatri.astype(jnp.bfloat16)
        parts_ref[:RANK, :] = high
        parts_ref[RANK:, :] = (khatri - high.astype(jnp.float32)).astype(jnp.bfloat16)

    base = pl.program_id(0) * per_step

    def joined(refs):
        return jnp.concatenate(
            [jnp.concatenate([ref[base + i] for ref in refs], axis=0) for i in range(per_step)], axis=1
        )

    both = jnp.dot(parts_ref[...], joined(weights[:PARTS]), preferred_element_type=jnp.float32)
    rest = jnp.dot(parts_ref[:RANK, :], joined(weights[PARTS:]), preferred_element_type=jnp.float32)
    total = both[:RANK] + (both[RANK:] + rest)
    most = jnp.max(jnp.abs(total), axis=1, keepdims=True)
    level = jnp.ceil(jnp.log2(jnp.maximum(most, 1e-35)) * STEP + 1.0)
    coded = jnp.round(total * jnp.exp2(level * (-1.0 / STEP)) * TOP).astype(jnp.int32).astype(jnp.int16)
    for i in range(per_step):
        out_ref[0, i * RANK : (i + 1) * RANK, :] = coded[:, i * LO : (i + 1) * LO]
    level_row = jnp.broadcast_to(level, (RANK, RANK)).T[:EXTRA]
    out_ref[0, per_step * RANK :, :] = level_row.astype(jnp.int32).astype(jnp.int16)


def products(item_at, word_at, count, pieces, highs, lows, me=None, interpret=False):
    per_step = OWN // LO
    sizes = [x.shape[0] // (2 * ROWS) for x in pieces]
    if not interpret:
        highs = [pltpu.with_memory_space_constraint(x, pltpu.VMEM) for x in highs]
        lows = [pltpu.with_memory_space_constraint(x, pltpu.VMEM) for x in lows]
    in_vmem = pl.BlockSpec(memory_space=pltpu.VMEM)
    return pl.pallas_call(
        functools.partial(product_body, sizes=sizes, per_step=per_step, me=me),
        grid_spec=pltpu.PrefetchScalarGridSpec(
            num_scalar_prefetch=3,
            grid=(PEERS,),
            in_specs=[in_vmem] * (len(pieces) + 2 * PARTS),
            out_specs=pl.BlockSpec((1, OWN + EXTRA, RANK), lambda i, *_: (i, 0, 0)),
            scratch_shapes=[
                pltpu.VMEM((PEERS * ROWS, RANK), jnp.float32),
                pltpu.VMEM((PEERS * ROWS, RANK), jnp.float32),
                pltpu.VMEM((TILES, RANK), jnp.float32),
                pltpu.VMEM((2 * RANK, TILES), jnp.bfloat16),
            ],
        ),
        out_shape=in_hbm((PEERS, OWN + EXTRA, RANK), jnp.int16, interpret),
        compiler_params=pltpu.CompilerParams(vmem_limit_bytes=20 * MIB),
        cost_estimate=pl.CostEstimate(flops=10 * 10**9, bytes_accessed=30 * 10**6, transcendentals=0),
        name="products",
        interpret=interpret,
    )(item_at, word_at, count, *pieces, *highs, *lows)


def finish_body(coded_ref, inverse_ref, out_ref, sum_ref):
    step = pl.program_id(0)

    @pl.when(step == 0)
    def _():
        sum_ref[...] = jnp.zeros_like(sum_ref)

    for j in range(FOLD):
        levels = coded_ref[j, OWN:, :].astype(jnp.int32).astype(jnp.float32)
        level = jnp.broadcast_to(levels[:1], (RANK, RANK)).T
        scale = jnp.exp2(level * (1.0 / STEP)) * (1.0 / TOP)
        for i in range(OWN // LO):
            part = coded_ref[j, i * RANK : (i + 1) * RANK, :].astype(jnp.int32).astype(jnp.float32)
            sum_ref[:, i * LO : (i + 1) * LO] += part * scale

    @pl.when(step == pl.num_programs(0) - 1)
    def _():
        out_ref[...] = lax.dot_general(
            sum_ref[...], inverse_ref[...], TN, precision=lax.Precision.HIGHEST, preferred_element_type=jnp.float32
        )


def finish(coded, inverse, interpret=False):
    return pl.pallas_call(
        finish_body,
        grid=(PEERS // FOLD,),
        in_specs=[
            pl.BlockSpec((FOLD, OWN + EXTRA, RANK), lambda i: (i, 0, 0)),
            pl.BlockSpec((RANK, RANK), lambda i: (0, 0)),
        ],
        out_specs=pl.BlockSpec((OWN, RANK), lambda i: (0, 0)),
        out_shape=jax.ShapeDtypeStruct((OWN, RANK), jnp.float32),
        scratch_shapes=[pltpu.VMEM((RANK, OWN), jnp.float32)],
        compiler_params=pltpu.CompilerParams(vmem_limit_bytes=20 * MIB),
        name="finish",
        interpret=interpret,
    )(coded, inverse)


def gram_body(*refs, me):
    pieces, out_ref, gram_ref = refs[:-2], refs[-2], refs[-1]
    mine = (lax.axis_index("rows") if me is None else me) % SLICES
    for i in range(2):
        x = jnp.concatenate(
            [ref[at : at + ROWS, :] for ref in pieces for at in range(i * ROWS, ref.shape[0], 2 * ROWS)], axis=0
        )
        gram_ref[...] = lax.dot_general(x, x, TN, preferred_element_type=jnp.float32)
        out_ref[i] = gram_ref[pl.ds(pl.multiple_of(mine * SLICE, SLICE), SLICE), :]


def partial_grams(pieces, me=None, interpret=False):
    return pl.pallas_call(
        functools.partial(gram_body, me=me),
        in_specs=[pl.BlockSpec(memory_space=pltpu.VMEM)] * len(pieces),
        out_specs=pl.BlockSpec(memory_space=pltpu.VMEM),
        out_shape=jax.ShapeDtypeStruct((2, SLICE, RANK), jnp.float32),
        scratch_shapes=[pltpu.VMEM((RANK, RANK), jnp.float32)],
        compiler_params=pltpu.CompilerParams(vmem_limit_bytes=20 * MIB),
        cost_estimate=pl.CostEstimate(flops=10**9, bytes_accessed=3 * 10**6, transcendentals=0),
        name="partial_grams",
        interpret=interpret,
    )(*pieces)


def fold_body(after_ref, a_ref, b_ref, c_ref, d_ref, out_ref):
    del after_ref
    out_ref[...] = (a_ref[...] + c_ref[...]) + (b_ref[...] + d_ref[...])


def folded(after, parts, interpret=False):
    in_vmem = pl.BlockSpec(memory_space=pltpu.VMEM)
    return pl.pallas_call(
        fold_body,
        in_specs=[pl.BlockSpec(memory_space=pl.ANY)] + [in_vmem] * 4,
        out_specs=in_vmem,
        out_shape=jax.ShapeDtypeStruct((2, SLICE, RANK), jnp.float32),
        compiler_params=pltpu.CompilerParams(vmem_limit_bytes=20 * MIB),
        name="folded",
        interpret=interpret,
    )(after, *parts)


def inverse_body(slices_ref, out_ref):
    slices = [sum(slices_ref[j] for j in range(i, PEERS, SLICES)) for i in range(SLICES)]
    a = jnp.concatenate([both[0] * both[1] for both in slices], axis=0)
    lane = lax.broadcasted_iota(jnp.int32, (1, RANK), 1)
    sublane = lax.broadcasted_iota(jnp.int32, (RANK, 1), 0)
    for k in range(0, RANK, PIVOTS):
        order = range(PIVOTS)
        rows = [a[k + i : k + i + 1, :] for i in order]
        block = [[jnp.broadcast_to(rows[i][:, k + j : k + j + 1], (1, RANK)) for j in order] for i in order]
        columns = [a[:, k + i : k + i + 1] for i in order]
        inside = (lane >= k) & (lane < k + PIVOTS)
        rows = [jnp.where(inside, jnp.where(lane == k + i, 1.0, 0.0), rows[i]) for i in order]
        for j in order:
            scale = 1.0 / block[j][j]
            for i in order:
                if i != j:
                    ratio = block[i][j] * scale
                    rows[i] = rows[i] - ratio * rows[j]
                    for n in range(j + 1, PIVOTS):
                        block[i][n] = block[i][n] - ratio * block[j][n]
            rows[j] = rows[j] * scale
            for n in range(j + 1, PIVOTS):
                block[j][n] = block[j][n] * scale
        a = jnp.where(inside, 0.0, a)
        for i in order:
            a = a - columns[i] * rows[i]
        for i in order:
            a = jnp.where(sublane == k + i, rows[i], a)
    out_ref[...] = a


def inverted(slices, interpret=False):
    return pl.pallas_call(
        inverse_body,
        grid=(1,),
        in_specs=[pl.BlockSpec((PEERS, 2, SLICE, RANK), lambda i: (0, 0, 0, 0))],
        out_specs=pl.BlockSpec((RANK, RANK), lambda i: (0, 0)),
        out_shape=jax.ShapeDtypeStruct((RANK, RANK), jnp.float32),
        cost_estimate=pl.CostEstimate(flops=10 * 10**9, bytes_accessed=30 * 10**6, transcendentals=0),
        compiler_params=pltpu.CompilerParams(vmem_limit_bytes=20 * MIB),
        name="inverted",
        interpret=interpret,
    )(slices)


def circled(x, along_y):
    def moved(k):
        dy, dx = (k, 0) if along_y else (0, k)
        return [(4 * y + x, 4 * ((y + dy) % 4) + (x + dx) % 4) for y in range(4) for x in range(4)]

    return [x] + [lax.ppermute(x, "cols", moved(k)) for k in (1, 2, 3)]


def on_device(values, tile_users, tile_items, tile_words, tile_count, factor_items, factor_words):
    across = [(i, i ^ 1) for i in range(PEERS)]
    around = [(2 * z, 2 * ((z + 1) % 8)) for z in range(8)] + [(2 * z + 1, 2 * ((z + 7) % 8) + 1) for z in range(8)]
    after = lax.optimization_barrier
    others = [lax.ppermute(x, "rows", across) for x in (factor_items, factor_words)]
    found = [jnp.concatenate([factor_items, factor_words, *others], axis=0)]
    highs, lows = [], []

    def build(arriving):
        high, low = build_weights(values, tile_users, len(highs), found[-1])
        arriving, low = after((arriving, low))
        highs.append(high)
        lows.append(low)
        return arriving

    found.append(build(build(lax.ppermute(found[-1], "rows", around))))
    arriving = lax.ppermute(found[-1], "rows", around)
    grams = circled(partial_grams(found), False)
    arriving, *grams = after((arriving, *grams))
    found.append(arriving)
    arriving = build(lax.ppermute(found[-1], "rows", around))
    grams = folded(found[-1], grams)
    arriving, grams = after((arriving, grams))
    found.append(arriving)
    arriving = lax.ppermute(found[-1][: 2 * ROWS], "rows", around)
    grams = circled(grams, True)
    arriving, *grams = after((build(arriving), *grams))
    found.append(arriving)
    pieces = found + [lax.ppermute(x, "rows", across) for x in found[1:]]
    coded = products(tile_items, tile_words, tile_count, pieces, highs, lows)
    summed = lax.all_to_all(coded, "cols", 0, 0)
    inverse = inverted(lax.all_gather(folded(coded, grams), "rows", axis=0))
    return finish(summed, inverse)


def solution(mesh):
    placed = (
        P(("rows", "cols"), None),
        P(("rows", "cols"), None),
        P(("rows", "cols")),
        P(("rows", "cols")),
        P(("rows", "cols")),
        P(("rows", "cols"), None),
        P(("rows", "cols"), None),
    )
    return jax.shard_map(
        on_device, mesh=mesh, in_specs=placed, out_specs=P(("rows", "cols"), None), check_vma=False
    )
```

```python
import functools

import jax
import jax.numpy as jnp
from jax import lax
from jax.experimental import pallas as pl
from jax.experimental.pallas import tpu as pltpu
from jax.sharding import PartitionSpec as P

RANK = 128
FIBER = 128
TILES = 512
ROWS = 256
OWN = 512
PEERS = 16
USERS = OWN * PEERS
LO = 128
HI = USERS // LO
EXTRA = 16
PARTS = 4
SLICES = 4
PIVOTS = 4
SLICE = RANK // SLICES
FOLD = 8
CHUNKS = 4
PART = TILES // PARTS
STEP = 128.0
TOP = 32767.0
NT = (((1,), (1,)), ((), ()))
TN = (((0,), (0,)), ((), ()))
MIB = 1024 * 1024


def in_hbm(shape, dtype, interpret):
    return jax.ShapeDtypeStruct(shape, dtype) if interpret else pltpu.HBM(shape, dtype)


def build_body(v_ref, u_ref, after_ref, high_ref, low_ref, acc_ref, *, block):
    del after_ref
    pitch = block + 1
    hi_iota = lax.broadcasted_iota(jnp.int32, (HI, FIBER), 0)
    lo_iota = lax.broadcasted_iota(jnp.int32, (LO, FIBER), 0)

    def add_block(g, carry):
        at = pl.multiple_of(g * block, block)
        for k in range(block):
            v = v_ref[pl.ds(at + k, 1), :]
            u = u_ref[pl.ds(at + k, 1), :]
            vh = v.astype(jnp.bfloat16).astype(jnp.float32)
            vl = v - vh
            hit = hi_iota == (u >> 7)
            left = jnp.concatenate(
                [jnp.where(hit, vh, 0.0).astype(jnp.bfloat16), jnp.where(hit, vl, 0.0).astype(jnp.bfloat16)], axis=1
            )
            one = jnp.where(lo_iota == (u & 127), 1.0, 0.0).astype(jnp.bfloat16)
            right = jnp.concatenate([one, one], axis=1)
            acc_ref[pl.ds(k, HI, stride=pitch), :] = lax.dot_general(
                left, right, NT, preferred_element_type=jnp.float32
            )
        for h in range(HI):
            weight = acc_ref[pl.ds(h * pitch, block), :]
            high = weight.astype(jnp.bfloat16)
            high_ref[h, pl.ds(at, block), :] = high
            low_ref[h, pl.ds(at, block), :] = (weight - high.astype(jnp.float32)).astype(jnp.bfloat16)
        return carry

    lax.fori_loop(0, PART // block, add_block, 0)


def build_weights(values, users, part, after, block=32, interpret=False):
    return pl.pallas_call(
        functools.partial(build_body, block=block),
        grid=(1,),
        in_specs=[pl.BlockSpec((PART, FIBER), lambda i: (part, 0))] * 2 + [pl.BlockSpec(memory_space=pl.ANY)],
        out_specs=[pl.BlockSpec(memory_space=pltpu.VMEM)] * 2,
        out_shape=[pltpu.VMEM((HI, PART, LO), jnp.bfloat16)] * 2 if not interpret else [jax.ShapeDtypeStruct((HI, PART, LO), jnp.bfloat16)] * 2,
        scratch_shapes=[pltpu.VMEM((HI * (block + 1), LO), jnp.float32)],
        compiler_params=pltpu.CompilerParams(vmem_limit_bytes=20 * MIB),
        cost_estimate=pl.CostEstimate(flops=6 * 10**9, bytes_accessed=20 * 10**6, transcendentals=0),
        name="build_weights",
        interpret=interpret,
    )(values, users, after)


def sources(me):
    z, c = me // 2, me % 2
    way = 1 - 2 * c
    blocks = [(z, c), (z, 1 - c)]
    for k in range(1, 4):
        blocks += [(z - k * way, c), (z - k * way, 1 - c)]
    blocks.append((z - 4 * way, c))
    for k in range(1, 4):
        blocks += [(z + k * way, 1 - c), (z + k * way, c)]
    blocks.append((z + 4 * way, 1 - c))
    return [(chip + 8) % 8 * 2 + core for chip, core in blocks]


def product_body(item_at, word_at, count, *refs, sizes, per_step, me):
    pieces = refs[: len(sizes)]
    weights = refs[len(sizes) : len(sizes) + 2 * PARTS]
    out_ref, item_ref, word_ref, khatri_ref, parts_ref = refs[len(sizes) + 2 * PARTS :]

    @pl.when(pl.program_id(0) == 0)
    def _():
        source = iter(sources(lax.axis_index("rows") if me is None else me))
        for ref, size in zip(pieces, sizes, strict=True):
            for j in range(size):
                at = pl.multiple_of(next(source) * ROWS, ROWS)
                item_ref[pl.ds(at, ROWS), :] = ref[2 * j * ROWS : (2 * j + 1) * ROWS, :].astype(jnp.float32)
                word_ref[pl.ds(at, ROWS), :] = ref[(2 * j + 1) * ROWS : (2 * j + 2) * ROWS, :].astype(jnp.float32)

        def take(g, carry):
            for k in range(16):
                t = g * 16 + k
                khatri_ref[pl.ds(t, 1), :] = item_ref[pl.ds(item_at[t], 1), :] * word_ref[pl.ds(word_at[t], 1), :]
            return carry

        lax.fori_loop(0, TILES // 16, take, 0)
        live = lax.broadcasted_iota(jnp.int32, (TILES, RANK), 0) < count[0]
        khatri = jnp.where(live, khatri_ref[...], 0.0).T
        high = khatri.astype(jnp.bfloat16)
        parts_ref[:RANK, :] = high
        parts_ref[RANK:, :] = (khatri - high.astype(jnp.float32)).astype(jnp.bfloat16)

    base = pl.program_id(0) * (per_step * CHUNKS)

    for chunk in range(CHUNKS):
        blocks = range(chunk * per_step, (chunk + 1) * per_step)

        def joined(refs, blocks=blocks):
            return jnp.concatenate([jnp.concatenate([ref[base + i] for ref in refs], axis=0) for i in blocks], axis=1)

        both = jnp.dot(parts_ref[...], joined(weights[:PARTS]), preferred_element_type=jnp.float32)
        rest = jnp.dot(parts_ref[:RANK, :], joined(weights[PARTS:]), preferred_element_type=jnp.float32)
        total = both[:RANK] + (both[RANK:] + rest)
        most = jnp.max(jnp.abs(total), axis=1, keepdims=True)
        level = jnp.ceil(jnp.log2(jnp.maximum(most, 1e-35)) * STEP + 1.0)
        coded = jnp.round(total * jnp.exp2(level * (-1.0 / STEP)) * TOP).astype(jnp.int32).astype(jnp.int16)
        for i in range(per_step):
            out_ref[chunk, i * RANK : (i + 1) * RANK, :] = coded[:, i * LO : (i + 1) * LO]
        level_row = jnp.broadcast_to(level, (RANK, RANK)).T[:EXTRA]
        out_ref[chunk, per_step * RANK :, :] = level_row.astype(jnp.int32).astype(jnp.int16)


def products(item_at, word_at, count, pieces, highs, lows, me=None, interpret=False):
    per_step = OWN // LO
    sizes = [x.shape[0] // (2 * ROWS) for x in pieces]
    if not interpret:
        highs = [pltpu.with_memory_space_constraint(x, pltpu.VMEM) for x in highs]
        lows = [pltpu.with_memory_space_constraint(x, pltpu.VMEM) for x in lows]
    in_vmem = pl.BlockSpec(memory_space=pltpu.VMEM)
    return pl.pallas_call(
        functools.partial(product_body, sizes=sizes, per_step=per_step, me=me),
        grid_spec=pltpu.PrefetchScalarGridSpec(
            num_scalar_prefetch=3,
            grid=(PEERS // CHUNKS,),
            in_specs=[in_vmem] * (len(pieces) + 2 * PARTS),
            out_specs=pl.BlockSpec((CHUNKS, OWN + EXTRA, RANK), lambda i, *_: (i, 0, 0)),
            scratch_shapes=[
                pltpu.VMEM((PEERS * ROWS, RANK), jnp.float32),
                pltpu.VMEM((PEERS * ROWS, RANK), jnp.float32),
                pltpu.VMEM((TILES, RANK), jnp.float32),
                pltpu.VMEM((2 * RANK, TILES), jnp.bfloat16),
            ],
        ),
        out_shape=in_hbm((PEERS, OWN + EXTRA, RANK), jnp.int16, interpret),
        compiler_params=pltpu.CompilerParams(vmem_limit_bytes=20 * MIB),
        cost_estimate=pl.CostEstimate(flops=10 * 10**9, bytes_accessed=30 * 10**6, transcendentals=0),
        name="products",
        interpret=interpret,
    )(item_at, word_at, count, *pieces, *highs, *lows)


def finish_body(coded_ref, inverse_ref, out_ref, sum_ref):
    step = pl.program_id(0)

    @pl.when(step == 0)
    def _():
        sum_ref[...] = jnp.zeros_like(sum_ref)

    for j in range(FOLD):
        levels = coded_ref[j, OWN:, :].astype(jnp.int32).astype(jnp.float32)
        level = jnp.broadcast_to(levels[:1], (RANK, RANK)).T
        scale = jnp.exp2(level * (1.0 / STEP)) * (1.0 / TOP)
        for i in range(OWN // LO):
            part = coded_ref[j, i * RANK : (i + 1) * RANK, :].astype(jnp.int32).astype(jnp.float32)
            sum_ref[:, i * LO : (i + 1) * LO] += part * scale

    @pl.when(step == pl.num_programs(0) - 1)
    def _():
        out_ref[...] = lax.dot_general(
            sum_ref[...], inverse_ref[...], TN, precision=lax.Precision.HIGHEST, preferred_element_type=jnp.float32
        )


def finish(coded, inverse, interpret=False):
    return pl.pallas_call(
        finish_body,
        grid=(PEERS // FOLD,),
        in_specs=[
            pl.BlockSpec((FOLD, OWN + EXTRA, RANK), lambda i: (i, 0, 0)),
            pl.BlockSpec((RANK, RANK), lambda i: (0, 0)),
        ],
        out_specs=pl.BlockSpec((OWN, RANK), lambda i: (0, 0)),
        out_shape=jax.ShapeDtypeStruct((OWN, RANK), jnp.float32),
        scratch_shapes=[pltpu.VMEM((RANK, OWN), jnp.float32)],
        compiler_params=pltpu.CompilerParams(vmem_limit_bytes=20 * MIB),
        name="finish",
        interpret=interpret,
    )(coded, inverse)


def gram_body(*refs, me):
    pieces, out_ref, gram_ref = refs[:-2], refs[-2], refs[-1]
    mine = (lax.axis_index("rows") if me is None else me) % SLICES
    for i in range(2):
        x = jnp.concatenate(
            [ref[at : at + ROWS, :] for ref in pieces for at in range(i * ROWS, ref.shape[0], 2 * ROWS)], axis=0
        )
        gram_ref[...] = lax.dot_general(x, x, TN, preferred_element_type=jnp.float32)
        out_ref[i] = gram_ref[pl.ds(pl.multiple_of(mine * SLICE, SLICE), SLICE), :]


def partial_grams(pieces, me=None, interpret=False):
    return pl.pallas_call(
        functools.partial(gram_body, me=me),
        in_specs=[pl.BlockSpec(memory_space=pltpu.VMEM)] * len(pieces),
        out_specs=pl.BlockSpec(memory_space=pltpu.VMEM),
        out_shape=jax.ShapeDtypeStruct((2, SLICE, RANK), jnp.float32),
        scratch_shapes=[pltpu.VMEM((RANK, RANK), jnp.float32)],
        compiler_params=pltpu.CompilerParams(vmem_limit_bytes=20 * MIB),
        cost_estimate=pl.CostEstimate(flops=10**9, bytes_accessed=3 * 10**6, transcendentals=0),
        name="partial_grams",
        interpret=interpret,
    )(*pieces)


def fold_body(after_ref, a_ref, b_ref, out_ref):
    del after_ref
    out_ref[...] = a_ref[...] + b_ref[...]


def folded(after, a, b, interpret=False):
    in_vmem = pl.BlockSpec(memory_space=pltpu.VMEM)
    return pl.pallas_call(
        fold_body,
        in_specs=[pl.BlockSpec(memory_space=pl.ANY), in_vmem, in_vmem],
        out_specs=in_vmem,
        out_shape=jax.ShapeDtypeStruct((2, SLICE, RANK), jnp.float32),
        compiler_params=pltpu.CompilerParams(vmem_limit_bytes=20 * MIB),
        name="folded",
        interpret=interpret,
    )(after, a, b)


def inverse_body(slices_ref, out_ref):
    slices = [sum(slices_ref[j] for j in range(i, PEERS, SLICES)) for i in range(SLICES)]
    a = jnp.concatenate([both[0] * both[1] for both in slices], axis=0)
    lane = lax.broadcasted_iota(jnp.int32, (1, RANK), 1)
    sublane = lax.broadcasted_iota(jnp.int32, (RANK, 1), 0)
    for k in range(0, RANK, PIVOTS):
        order = range(PIVOTS)
        rows = [a[k + i : k + i + 1, :] for i in order]
        block = [[jnp.broadcast_to(rows[i][:, k + j : k + j + 1], (1, RANK)) for j in order] for i in order]
        columns = [a[:, k + i : k + i + 1] for i in order]
        inside = (lane >= k) & (lane < k + PIVOTS)
        rows = [jnp.where(inside, jnp.where(lane == k + i, 1.0, 0.0), rows[i]) for i in order]
        for j in order:
            scale = 1.0 / block[j][j]
            for i in order:
                if i != j:
                    ratio = block[i][j] * scale
                    rows[i] = rows[i] - ratio * rows[j]
                    for n in range(j + 1, PIVOTS):
                        block[i][n] = block[i][n] - ratio * block[j][n]
            rows[j] = rows[j] * scale
            for n in range(j + 1, PIVOTS):
                block[j][n] = block[j][n] * scale
        a = jnp.where(inside, 0.0, a)
        for i in order:
            a = a - columns[i] * rows[i]
        for i in order:
            a = jnp.where(sublane == k + i, rows[i], a)
    out_ref[...] = a


def inverted(slices, interpret=False):
    return pl.pallas_call(
        inverse_body,
        grid=(1,),
        in_specs=[pl.BlockSpec((PEERS, 2, SLICE, RANK), lambda i: (0, 0, 0, 0))],
        out_specs=pl.BlockSpec((RANK, RANK), lambda i: (0, 0)),
        out_shape=jax.ShapeDtypeStruct((RANK, RANK), jnp.float32),
        cost_estimate=pl.CostEstimate(flops=10 * 10**9, bytes_accessed=30 * 10**6, transcendentals=0),
        compiler_params=pltpu.CompilerParams(vmem_limit_bytes=20 * MIB),
        name="inverted",
        interpret=interpret,
    )(slices)


def on_device(values, tile_users, tile_items, tile_words, tile_count, factor_items, factor_words):
    across = [(i, i ^ 1) for i in range(PEERS)]
    around = [(2 * z, 2 * ((z + 1) % 8)) for z in range(8)] + [(2 * z + 1, 2 * ((z + 7) % 8) + 1) for z in range(8)]
    after = lax.optimization_barrier
    others = [lax.ppermute(x, "rows", across) for x in (factor_items, factor_words)]
    found = [jnp.concatenate([factor_items, factor_words, *others], axis=0)]
    highs, lows = [], []
    grams = None
    for step in range(4):
        arriving = lax.ppermute(found[-1] if step < 3 else found[-1][: 2 * ROWS], "rows", around)
        if step:
            grams = partial_grams(found) if step == 1 else folded(found[-1], grams, more)
            more = lax.ppermute(grams, "cols", [(i, i ^ (1 << (step - 1))) for i in range(PEERS)])
        high, low = build_weights(values, tile_users, step, found[-1])
        if step:
            arriving, low, more = after((arriving, low, more))
        else:
            arriving, low = after((arriving, low))
        highs.append(high)
        lows.append(low)
        found.append(arriving)
    grams = folded(found[-1], grams, more)
    more = lax.ppermute(grams, "cols", [(i, i ^ 8) for i in range(PEERS)])
    pieces = found + [lax.ppermute(x, "rows", across) for x in found[1:]]
    coded = products(tile_items, tile_words, tile_count, pieces, highs, lows)
    coded, more = after((coded, more))
    summed = lax.all_to_all(coded, "cols", 0, 0)
    inverse = inverted(lax.all_gather(folded(coded, grams, more), "rows", axis=0))
    return finish(summed, inverse)


def solution(mesh):
    placed = (
        P(("rows", "cols"), None),
        P(("rows", "cols"), None),
        P(("rows", "cols")),
        P(("rows", "cols")),
        P(("rows", "cols")),
        P(("rows", "cols"), None),
        P(("rows", "cols"), None),
    )
    return jax.shard_map(
        on_device, mesh=mesh, in_specs=placed, out_specs=P(("rows", "cols"), None), check_vma=False
    )
```

```python
import functools

import jax
import jax.numpy as jnp
from jax import lax
from jax.experimental import pallas as pl
from jax.experimental.pallas import tpu as pltpu
from jax.sharding import PartitionSpec as P

RANK = 128
FIBER = 128
TILES = 512
ROWS = 256
OWN = 512
PEERS = 16
USERS = OWN * PEERS
LO = 128
HI = USERS // LO
EXTRA = 16
PARTS = 4
SLICES = 2
PIVOTS = 4
SLICE = RANK // SLICES
SIDE = 4
TILES_OWN = OWN // LO
PART = TILES // PARTS
STEP = 128.0
TOP = 32767.0
NT = (((1,), (1,)), ((), ()))
TN = (((0,), (0,)), ((), ()))
MIB = 1024 * 1024


def in_hbm(shape, dtype, interpret):
    return jax.ShapeDtypeStruct(shape, dtype) if interpret else pltpu.HBM(shape, dtype)


def build_body(v_ref, u_ref, after_ref, high_ref, low_ref, acc_ref, *, block):
    del after_ref
    pitch = block + 1
    hi_iota = lax.broadcasted_iota(jnp.int32, (HI, FIBER), 0)
    lo_iota = lax.broadcasted_iota(jnp.int32, (LO, FIBER), 0)

    def add_block(g, carry):
        at = pl.multiple_of(g * block, block)
        for k in range(block):
            v = v_ref[pl.ds(at + k, 1), :]
            u = u_ref[pl.ds(at + k, 1), :]
            vh = v.astype(jnp.bfloat16).astype(jnp.float32)
            vl = v - vh
            hit = hi_iota == (u >> 7)
            left = jnp.concatenate(
                [jnp.where(hit, vh, 0.0).astype(jnp.bfloat16), jnp.where(hit, vl, 0.0).astype(jnp.bfloat16)], axis=1
            )
            one = jnp.where(lo_iota == (u & 127), 1.0, 0.0).astype(jnp.bfloat16)
            right = jnp.concatenate([one, one], axis=1)
            acc_ref[pl.ds(k, HI, stride=pitch), :] = lax.dot_general(
                left, right, NT, preferred_element_type=jnp.float32
            )
        for h in range(HI):
            weight = acc_ref[pl.ds(h * pitch, block), :]
            high = weight.astype(jnp.bfloat16)
            high_ref[h, pl.ds(at, block), :] = high
            low_ref[h, pl.ds(at, block), :] = (weight - high.astype(jnp.float32)).astype(jnp.bfloat16)
        return carry

    lax.fori_loop(0, PART // block, add_block, 0)


def build_weights(values, users, part, after, block=32, interpret=False):
    return pl.pallas_call(
        functools.partial(build_body, block=block),
        grid=(1,),
        in_specs=[pl.BlockSpec((PART, FIBER), lambda i: (part, 0))] * 2 + [pl.BlockSpec(memory_space=pl.ANY)],
        out_specs=[pl.BlockSpec(memory_space=pltpu.VMEM)] * 2,
        out_shape=[pltpu.VMEM((HI, PART, LO), jnp.bfloat16)] * 2 if not interpret else [jax.ShapeDtypeStruct((HI, PART, LO), jnp.bfloat16)] * 2,
        scratch_shapes=[pltpu.VMEM((HI * (block + 1), LO), jnp.float32)],
        compiler_params=pltpu.CompilerParams(vmem_limit_bytes=20 * MIB),
        cost_estimate=pl.CostEstimate(flops=6 * 10**9, bytes_accessed=20 * 10**6, transcendentals=0),
        name="build_weights",
        interpret=interpret,
    )(values, users, after)


def sources(me):
    z, c = me // 2, me % 2
    way = 1 - 2 * c
    blocks = [(z, c), (z, 1 - c)]
    for k in range(1, 4):
        blocks += [(z - k * way, c), (z - k * way, 1 - c)]
    blocks.append((z - 4 * way, c))
    for k in range(1, 4):
        blocks += [(z + k * way, 1 - c), (z + k * way, c)]
    blocks.append((z + 4 * way, 1 - c))
    return [(chip + 8) % 8 * 2 + core for chip, core in blocks]


def encode(total, store, base):
    most = jnp.max(jnp.abs(total), axis=1, keepdims=True)
    level = jnp.ceil(jnp.log2(jnp.maximum(most, 1e-35)) * STEP + 1.0)
    coded = jnp.round(total * jnp.exp2(level * (-1.0 / STEP)) * TOP).astype(jnp.int32).astype(jnp.int16)
    for i in range(total.shape[1] // LO):
        store[base + i * RANK : base + (i + 1) * RANK, :] = coded[:, i * LO : (i + 1) * LO]
    return jnp.broadcast_to(level, (RANK, RANK)).T[:EXTRA]


def decode(ref, base, tiles, levels):
    level = jnp.broadcast_to(levels, (RANK, RANK)).T
    scale = jnp.exp2(level * (1.0 / STEP)) * (1.0 / TOP)
    return jnp.concatenate(
        [
            ref[base + i * RANK : base + (i + 1) * RANK, :].astype(jnp.int32).astype(jnp.float32) * scale
            for i in range(tiles)
        ],
        axis=1,
    )


def place(me):
    at = lax.axis_index("cols") if me is None else me
    return at // SIDE, at % SIDE


def product_body(*refs, along_x, sizes, me, at):
    first = sizes is not None
    if first:
        item_at, word_at, count = refs[:3]
        pieces = refs[3 : 3 + len(sizes)]
        refs = refs[3 + len(sizes) :]
    else:
        parts_ref, refs = refs[0], refs[1:]
    weights, refs = refs[: 2 * PARTS], refs[2 * PARTS :]
    outs, own_ref = refs[: SIDE - 1], refs[SIDE - 1]
    if first:
        parts_ref, item_ref, word_ref, khatri_ref = refs[SIDE:]
        source = iter(sources(lax.axis_index("rows") if me is None else me))
        for ref, size in zip(pieces, sizes, strict=True):
            for j in range(size):
                row = pl.multiple_of(next(source) * ROWS, ROWS)
                item_ref[pl.ds(row, ROWS), :] = ref[2 * j * ROWS : (2 * j + 1) * ROWS, :].astype(jnp.float32)
                word_ref[pl.ds(row, ROWS), :] = ref[(2 * j + 1) * ROWS : (2 * j + 2) * ROWS, :].astype(jnp.float32)

        def take(g, carry):
            for k in range(16):
                t = g * 16 + k
                khatri_ref[pl.ds(t, 1), :] = item_ref[pl.ds(item_at[t], 1), :] * word_ref[pl.ds(word_at[t], 1), :]
            return carry

        lax.fori_loop(0, TILES // 16, take, 0)
        live = lax.broadcasted_iota(jnp.int32, (TILES, RANK), 0) < count[0]
        khatri = jnp.where(live, khatri_ref[...], 0.0).T
        high = khatri.astype(jnp.bfloat16)
        parts_ref[:RANK, :] = high
        parts_ref[RANK:, :] = (khatri - high.astype(jnp.float32)).astype(jnp.bfloat16)

    y, x = place(at)
    half = 0 if along_x else TILES_OWN // 2
    for k in (1, 2, 3, 0):
        rows = []
        for other in range(SIDE):
            owner = other * SIDE + (x + k) % SIDE if along_x else (y + k) % SIDE * SIDE + other
            base = owner * TILES_OWN + half

            def joined(refs, base=base):
                return jnp.concatenate(
                    [jnp.concatenate([ref[base + i] for ref in refs], axis=0) for i in range(TILES_OWN // 2)], axis=1
                )

            both = jnp.dot(parts_ref[...], joined(weights[:PARTS]), preferred_element_type=jnp.float32)
            rest = jnp.dot(parts_ref[:RANK, :], joined(weights[PARTS:]), preferred_element_type=jnp.float32)
            total = both[:RANK] + (both[RANK:] + rest)
            if k:
                rows.append(encode(total, outs[k - 1], other * (OWN // 2)))
            else:
                own_ref[other] = total
        if k:
            levels = jnp.concatenate([row[:1] for row in rows] + [rows[0][: EXTRA - SIDE]], axis=0)
            outs[k - 1][SIDE * OWN // 2 :, :] = levels.astype(jnp.int32).astype(jnp.int16)


def products(along_x, highs, lows, *, parts=None, pieces=None, scalars=None, me=None, at=None, interpret=False):
    if not interpret:
        highs = [pltpu.with_memory_space_constraint(x, pltpu.VMEM) for x in highs]
        lows = [pltpu.with_memory_space_constraint(x, pltpu.VMEM) for x in lows]
    in_vmem = pl.BlockSpec(memory_space=pltpu.VMEM)
    first = parts is None
    sizes = [x.shape[0] // (2 * ROWS) for x in pieces] if first else None
    operands = (*scalars, *pieces) if first else (parts,)
    in_specs = [pl.BlockSpec(memory_space=pltpu.SMEM)] * 3 + [in_vmem] * len(pieces) if first else [in_vmem]
    out_shape = [jax.ShapeDtypeStruct((SIDE * OWN // 2 + EXTRA, LO), jnp.int16)] * (SIDE - 1)
    out_shape.append(jax.ShapeDtypeStruct((SIDE, RANK, OWN // 2), jnp.float32))
    scratch = []
    if first:
        out_shape.append(jax.ShapeDtypeStruct((2 * RANK, TILES), jnp.bfloat16))
        scratch = [pltpu.VMEM((PEERS * ROWS, RANK), jnp.float32)] * 2 + [pltpu.VMEM((TILES, RANK), jnp.float32)]
    return pl.pallas_call(
        functools.partial(product_body, along_x=along_x, sizes=sizes, me=me, at=at),
        in_specs=in_specs + [in_vmem] * (2 * PARTS),
        out_specs=[in_vmem] * len(out_shape),
        out_shape=out_shape,
        scratch_shapes=scratch,
        compiler_params=pltpu.CompilerParams(vmem_limit_bytes=24 * MIB),
        cost_estimate=pl.CostEstimate(flops=4 * 10**9, bytes_accessed=13 * 10**6, transcendentals=0),
        name="products",
        interpret=interpret,
    )(*operands, *highs, *lows)


def relay_body(own_ref, a_ref, b_ref, c_ref, *refs, along_x, at):
    outs, mine_ref, sum_ref = refs[: SIDE - 1], refs[SIDE - 1], refs[SIDE]
    width = OWN // 2
    for other in range(SIDE):
        total = own_ref[other]
        for ref in (a_ref, b_ref, c_ref):
            levels = ref[SIDE * width :, :].astype(jnp.int32).astype(jnp.float32)
            total = total + decode(ref, other * width, width // LO, levels[other : other + 1])
        sum_ref[other] = total
    y, x = place(at)
    for k in range(SIDE):
        total = sum_ref[((y if along_x else x) + k) % SIDE]
        if k:
            outs[k - 1][width:, :] = encode(total, outs[k - 1], 0).astype(jnp.int32).astype(jnp.int16)
        else:
            mine_ref[...] = total


def relayed(along_x, own, received, at=None, interpret=False):
    in_vmem = pl.BlockSpec(memory_space=pltpu.VMEM)
    return pl.pallas_call(
        functools.partial(relay_body, along_x=along_x, at=at),
        in_specs=[in_vmem] * SIDE,
        out_specs=[in_vmem] * SIDE,
        out_shape=[jax.ShapeDtypeStruct((OWN // 2 + EXTRA, LO), jnp.int16)] * (SIDE - 1)
        + [jax.ShapeDtypeStruct((RANK, OWN // 2), jnp.float32)],
        scratch_shapes=[pltpu.VMEM((SIDE, RANK, OWN // 2), jnp.float32)],
        compiler_params=pltpu.CompilerParams(vmem_limit_bytes=20 * MIB),
        cost_estimate=pl.CostEstimate(flops=2 * 10**9, bytes_accessed=7 * 10**6, transcendentals=0),
        name="relayed",
        interpret=interpret,
    )(own, *received)


def finish_body(*refs):
    inverse_ref, out_ref = refs[2 * SIDE :]
    width = OWN // 2
    sums = []
    for own_ref, *received in (refs[:SIDE], refs[SIDE : 2 * SIDE]):
        total = own_ref[...]
        for ref in received:
            levels = ref[width:, :].astype(jnp.int32).astype(jnp.float32)
            total = total + decode(ref, 0, width // LO, levels[:1])
        sums.append(total)
    out_ref[...] = lax.dot_general(
        jnp.concatenate(sums, axis=1),
        inverse_ref[...],
        TN,
        precision=lax.Precision.HIGHEST,
        preferred_element_type=jnp.float32,
    )


def finish(first, second, inverse, interpret=False):
    in_vmem = pl.BlockSpec(memory_space=pltpu.VMEM)
    return pl.pallas_call(
        finish_body,
        in_specs=[in_vmem] * (2 * SIDE + 1),
        out_specs=in_vmem,
        out_shape=jax.ShapeDtypeStruct((OWN, RANK), jnp.float32),
        compiler_params=pltpu.CompilerParams(vmem_limit_bytes=20 * MIB),
        name="finish",
        interpret=interpret,
    )(*first, *second, inverse)


def gram_body(*refs, me):
    pieces, out_ref, gram_ref = refs[:-2], refs[-2], refs[-1]
    mine = (lax.axis_index("rows") if me is None else me) % SLICES
    for i in range(2):
        x = jnp.concatenate(
            [ref[at : at + ROWS, :] for ref in pieces for at in range(i * ROWS, ref.shape[0], 2 * ROWS)], axis=0
        )
        gram_ref[...] = lax.dot_general(x, x, TN, preferred_element_type=jnp.float32)
        out_ref[i] = gram_ref[pl.ds(pl.multiple_of(mine * SLICE, SLICE), SLICE), :]


def partial_grams(pieces, me=None, interpret=False):
    return pl.pallas_call(
        functools.partial(gram_body, me=me),
        in_specs=[pl.BlockSpec(memory_space=pltpu.VMEM)] * len(pieces),
        out_specs=pl.BlockSpec(memory_space=pltpu.VMEM),
        out_shape=jax.ShapeDtypeStruct((2, SLICE, RANK), jnp.float32),
        scratch_shapes=[pltpu.VMEM((RANK, RANK), jnp.float32)],
        compiler_params=pltpu.CompilerParams(vmem_limit_bytes=20 * MIB),
        cost_estimate=pl.CostEstimate(flops=10**9, bytes_accessed=3 * 10**6, transcendentals=0),
        name="partial_grams",
        interpret=interpret,
    )(*pieces)


def fold_body(after_ref, a_ref, b_ref, out_ref, *, multiply):
    del after_ref
    if multiply:
        out_ref[...] = (a_ref[0] + b_ref[0]) * (a_ref[1] + b_ref[1])
    else:
        out_ref[...] = a_ref[...] + b_ref[...]


def folded(after, a, b, multiply=False, interpret=False):
    in_vmem = pl.BlockSpec(memory_space=pltpu.VMEM)
    return pl.pallas_call(
        functools.partial(fold_body, multiply=multiply),
        in_specs=[pl.BlockSpec(memory_space=pl.ANY), in_vmem, in_vmem],
        out_specs=in_vmem,
        out_shape=jax.ShapeDtypeStruct(a.shape[1:] if multiply else a.shape, jnp.float32),
        compiler_params=pltpu.CompilerParams(vmem_limit_bytes=20 * MIB),
        name="folded",
        interpret=interpret,
    )(after, a, b)


def inverse_body(mine_ref, other_ref, out_ref, gram_ref, *, me):
    core = (lax.axis_index("rows") if me is None else me) % 2
    gram_ref[pl.ds(pl.multiple_of(core * SLICE, SLICE), SLICE), :] = mine_ref[...]
    gram_ref[pl.ds(pl.multiple_of((1 - core) * SLICE, SLICE), SLICE), :] = other_ref[...]
    a = gram_ref[...]
    lane = lax.broadcasted_iota(jnp.int32, (1, RANK), 1)
    sublane = lax.broadcasted_iota(jnp.int32, (RANK, 1), 0)
    for k in range(0, RANK, PIVOTS):
        order = range(PIVOTS)
        rows = [a[k + i : k + i + 1, :] for i in order]
        block = [[jnp.broadcast_to(rows[i][:, k + j : k + j + 1], (1, RANK)) for j in order] for i in order]
        columns = [a[:, k + i : k + i + 1] for i in order]
        inside = (lane >= k) & (lane < k + PIVOTS)
        rows = [jnp.where(inside, jnp.where(lane == k + i, 1.0, 0.0), rows[i]) for i in order]
        for j in order:
            scale = 1.0 / block[j][j]
            for i in order:
                if i != j:
                    ratio = block[i][j] * scale
                    rows[i] = rows[i] - ratio * rows[j]
                    for n in range(j + 1, PIVOTS):
                        block[i][n] = block[i][n] - ratio * block[j][n]
            rows[j] = rows[j] * scale
            for n in range(j + 1, PIVOTS):
                block[j][n] = block[j][n] * scale
        a = jnp.where(inside, 0.0, a)
        for i in order:
            a = a - columns[i] * rows[i]
        for i in order:
            a = jnp.where(sublane == k + i, rows[i], a)
    out_ref[...] = a


def inverted(mine, other, me=None, interpret=False):
    in_vmem = pl.BlockSpec(memory_space=pltpu.VMEM)
    return pl.pallas_call(
        functools.partial(inverse_body, me=me),
        in_specs=[in_vmem, in_vmem],
        out_specs=in_vmem,
        out_shape=jax.ShapeDtypeStruct((RANK, RANK), jnp.float32),
        scratch_shapes=[pltpu.VMEM((RANK, RANK), jnp.float32)],
        compiler_params=pltpu.CompilerParams(vmem_limit_bytes=20 * MIB),
        cost_estimate=pl.CostEstimate(flops=4 * 10**9, bytes_accessed=15 * 10**6, transcendentals=0),
        name="inverted",
        interpret=interpret,
    )(mine, other)


def swapped(bits):
    return [(i, i ^ bits) for i in range(PEERS)]


def along(xs, along_x):
    def moved(k):
        dy, dx = (0, k) if along_x else (k, 0)
        return [(SIDE * y + x, SIDE * ((y + dy) % SIDE) + (x + dx) % SIDE) for y in range(SIDE) for x in range(SIDE)]

    last, first, second = (lax.ppermute(xs[k - 1], "cols", moved(k)) for k in (2, 1, 3))
    return [first, last, second]


def on_device(values, tile_users, tile_items, tile_words, tile_count, factor_items, factor_words):
    across = swapped(1)
    around = [(2 * z, 2 * ((z + 1) % 8)) for z in range(8)] + [(2 * z + 1, 2 * ((z + 7) % 8) + 1) for z in range(8)]
    after = lax.optimization_barrier
    others = [lax.ppermute(x, "rows", across) for x in (factor_items, factor_words)]
    found = [jnp.concatenate([factor_items, factor_words, *others], axis=0)]
    highs, lows = [], []
    grams = partial_grams(found)
    more = lax.ppermute(grams, "cols", swapped(1))
    for step in range(4):
        arriving = lax.ppermute(found[-1] if step < 3 else found[-1][: 2 * ROWS], "rows", around)
        high, low = build_weights(values, tile_users, step, found[-1])
        if step == 0:
            grams = folded(found[-1], grams, more)
            arriving, low, grams = after((arriving, low, grams))
            more = lax.ppermute(grams, "cols", swapped(2))
        else:
            grams = folded(found[-1], grams, more)
            more = lax.ppermute(grams, *(("cols", swapped(2 << step)) if step < 3 else ("rows", swapped(2))))
            arriving, low, more = after((arriving, low, more))
        highs.append(high)
        lows.append(low)
        found.append(arriving)
    pieces = found + [lax.ppermute(x, "rows", across) for x in found[1:]]
    scalars = (tile_items, tile_words, tile_count)
    *out, own_a, parts = products(True, highs, lows, pieces=pieces, scalars=scalars)
    in_a = along(out, True)
    *out, own_b = products(False, highs, lows, parts=parts)
    in_b = along(out, False)
    grams = folded(own_b, grams, more)
    more = lax.ppermute(grams, "rows", swapped(4))
    own_a, more = after((own_a, more))
    *out, own_a = relayed(True, own_a, in_a)
    end_a = along(out, False)
    grams = folded(own_a, grams, more)
    more = lax.ppermute(grams, "rows", swapped(8))
    *out, own_b = relayed(False, own_b, in_b)
    end_b = along(out, True)
    grams = folded(own_b, grams, more, multiply=True)
    inverse = inverted(grams, lax.ppermute(grams, "rows", across))
    return finish((own_a, *end_a), (own_b, *end_b), inverse)


def solution(mesh):
    placed = (
        P(("rows", "cols"), None),
        P(("rows", "cols"), None),
        P(("rows", "cols")),
        P(("rows", "cols")),
        P(("rows", "cols")),
        P(("rows", "cols"), None),
        P(("rows", "cols"), None),
    )
    return jax.shard_map(
        on_device, mesh=mesh, in_specs=placed, out_specs=P(("rows", "cols"), None), check_vma=False
    )
```

```python
import functools

import jax
import jax.numpy as jnp
from jax import lax
from jax.experimental import pallas as pl
from jax.experimental.pallas import tpu as pltpu
from jax.sharding import PartitionSpec as P

RANK = 128
FIBER = 128
TILES = 512
ROWS = 256
OWN = 512
PEERS = 16
USERS = OWN * PEERS
LO = 128
HI = USERS // LO
EXTRA = 16
PARTS = 4
SLICES = 2
PIVOTS = 4
SLICE = RANK // SLICES
SIDE = 4
TILES_OWN = OWN // LO
PART = TILES // PARTS
STEP = 128.0
TOP = 32767.0
NT = (((1,), (1,)), ((), ()))
TN = (((0,), (0,)), ((), ()))
MIB = 1024 * 1024


def in_hbm(shape, dtype, interpret):
    return jax.ShapeDtypeStruct(shape, dtype) if interpret else pltpu.HBM(shape, dtype)


def build_body(v_ref, u_ref, after_ref, high_ref, low_ref, acc_ref, *, block):
    del after_ref
    pitch = block + 1
    hi_iota = lax.broadcasted_iota(jnp.int32, (HI, FIBER), 0)
    lo_iota = lax.broadcasted_iota(jnp.int32, (LO, FIBER), 0)

    def add_block(g, carry):
        at = pl.multiple_of(g * block, block)
        for k in range(block):
            v = v_ref[pl.ds(at + k, 1), :]
            u = u_ref[pl.ds(at + k, 1), :]
            vh = v.astype(jnp.bfloat16).astype(jnp.float32)
            vl = v - vh
            hit = hi_iota == (u >> 7)
            left = jnp.concatenate(
                [jnp.where(hit, vh, 0.0).astype(jnp.bfloat16), jnp.where(hit, vl, 0.0).astype(jnp.bfloat16)], axis=1
            )
            one = jnp.where(lo_iota == (u & 127), 1.0, 0.0).astype(jnp.bfloat16)
            right = jnp.concatenate([one, one], axis=1)
            acc_ref[pl.ds(k, HI, stride=pitch), :] = lax.dot_general(
                left, right, NT, preferred_element_type=jnp.float32
            )
        for h in range(HI):
            weight = acc_ref[pl.ds(h * pitch, block), :]
            high = weight.astype(jnp.bfloat16)
            high_ref[h, pl.ds(at, block), :] = high
            low_ref[h, pl.ds(at, block), :] = (weight - high.astype(jnp.float32)).astype(jnp.bfloat16)
        return carry

    lax.fori_loop(0, PART // block, add_block, 0)


def build_weights(values, users, part, after, block=32, interpret=False):
    return pl.pallas_call(
        functools.partial(build_body, block=block),
        grid=(1,),
        in_specs=[pl.BlockSpec((PART, FIBER), lambda i: (part, 0))] * 2 + [pl.BlockSpec(memory_space=pl.ANY)],
        out_specs=[pl.BlockSpec(memory_space=pltpu.VMEM)] * 2,
        out_shape=[pltpu.VMEM((HI, PART, LO), jnp.bfloat16)] * 2 if not interpret else [jax.ShapeDtypeStruct((HI, PART, LO), jnp.bfloat16)] * 2,
        scratch_shapes=[pltpu.VMEM((HI * (block + 1), LO), jnp.float32)],
        compiler_params=pltpu.CompilerParams(vmem_limit_bytes=20 * MIB),
        cost_estimate=pl.CostEstimate(flops=6 * 10**9, bytes_accessed=20 * 10**6, transcendentals=0),
        name="build_weights",
        interpret=interpret,
    )(values, users, after)


def sources(me):
    z, c = me // 2, me % 2
    way = 1 - 2 * c
    blocks = [(z, c), (z, 1 - c)]
    for k in range(1, 4):
        blocks += [(z - k * way, c), (z - k * way, 1 - c)]
    blocks.append((z - 4 * way, c))
    for k in range(1, 4):
        blocks += [(z + k * way, 1 - c), (z + k * way, c)]
    blocks.append((z + 4 * way, 1 - c))
    return [(chip + 8) % 8 * 2 + core for chip, core in blocks]


def encode(total, store, base):
    most = jnp.max(jnp.abs(total), axis=1, keepdims=True)
    level = jnp.ceil(jnp.log2(jnp.maximum(most, 1e-35)) * STEP + 1.0)
    coded = jnp.round(total * jnp.exp2(level * (-1.0 / STEP)) * TOP).astype(jnp.int32).astype(jnp.int16)
    for i in range(total.shape[1] // LO):
        store[base + i * RANK : base + (i + 1) * RANK, :] = coded[:, i * LO : (i + 1) * LO]
    return jnp.broadcast_to(level, (RANK, RANK)).T[:EXTRA]


def decode(ref, base, tiles, levels):
    level = jnp.broadcast_to(levels, (RANK, RANK)).T
    scale = jnp.exp2(level * (1.0 / STEP)) * (1.0 / TOP)
    return jnp.concatenate(
        [
            ref[base + i * RANK : base + (i + 1) * RANK, :].astype(jnp.int32).astype(jnp.float32) * scale
            for i in range(tiles)
        ],
        axis=1,
    )


def place(me):
    at = lax.axis_index("cols") if me is None else me
    return at // SIDE, at % SIDE


def product_body(*refs, along_x, sizes, me, at):
    first = sizes is not None
    if first:
        item_at, word_at, count = refs[:3]
        pieces = refs[3 : 3 + len(sizes)]
        refs = refs[3 + len(sizes) :]
    else:
        parts_ref, refs = refs[0], refs[1:]
    weights, refs = refs[: 2 * PARTS], refs[2 * PARTS :]
    outs, own_ref = refs[: SIDE - 1], refs[SIDE - 1]
    if first:
        parts_ref, item_ref, word_ref, khatri_ref = refs[SIDE:]
        source = iter(sources(lax.axis_index("rows") if me is None else me))
        for ref, size in zip(pieces, sizes, strict=True):
            for j in range(size):
                row = pl.multiple_of(next(source) * ROWS, ROWS)
                item_ref[pl.ds(row, ROWS), :] = ref[2 * j * ROWS : (2 * j + 1) * ROWS, :].astype(jnp.float32)
                word_ref[pl.ds(row, ROWS), :] = ref[(2 * j + 1) * ROWS : (2 * j + 2) * ROWS, :].astype(jnp.float32)

        def take(g, carry):
            for k in range(16):
                t = g * 16 + k
                khatri_ref[pl.ds(t, 1), :] = item_ref[pl.ds(item_at[t], 1), :] * word_ref[pl.ds(word_at[t], 1), :]
            return carry

        lax.fori_loop(0, TILES // 16, take, 0)
        live = lax.broadcasted_iota(jnp.int32, (TILES, RANK), 0) < count[0]
        khatri = jnp.where(live, khatri_ref[...], 0.0).T
        high = khatri.astype(jnp.bfloat16)
        parts_ref[:RANK, :] = high
        parts_ref[RANK:, :] = (khatri - high.astype(jnp.float32)).astype(jnp.bfloat16)

    y, x = place(at)
    half = 0 if along_x else TILES_OWN // 2
    for k in (1, 2, 3, 0):
        rows = []
        for other in range(SIDE):
            owner = other * SIDE + (x + k) % SIDE if along_x else (y + k) % SIDE * SIDE + other
            base = owner * TILES_OWN + half

            def joined(refs, base=base):
                return jnp.concatenate(
                    [jnp.concatenate([ref[base + i] for ref in refs], axis=0) for i in range(TILES_OWN // 2)], axis=1
                )

            both = jnp.dot(parts_ref[...], joined(weights[:PARTS]), preferred_element_type=jnp.float32)
            rest = jnp.dot(parts_ref[:RANK, :], joined(weights[PARTS:]), preferred_element_type=jnp.float32)
            total = both[:RANK] + (both[RANK:] + rest)
            if k:
                rows.append(encode(total, outs[k - 1], other * (OWN // 2)))
            else:
                own_ref[other] = total
        if k:
            levels = jnp.concatenate([row[:1] for row in rows] + [rows[0][: EXTRA - SIDE]], axis=0)
            outs[k - 1][SIDE * OWN // 2 :, :] = levels.astype(jnp.int32).astype(jnp.int16)


def products(along_x, highs, lows, *, parts=None, pieces=None, scalars=None, me=None, at=None, interpret=False):
    if not interpret:
        highs = [pltpu.with_memory_space_constraint(x, pltpu.VMEM) for x in highs]
        lows = [pltpu.with_memory_space_constraint(x, pltpu.VMEM) for x in lows]
    in_vmem = pl.BlockSpec(memory_space=pltpu.VMEM)
    first = parts is None
    sizes = [x.shape[0] // (2 * ROWS) for x in pieces] if first else None
    operands = (*scalars, *pieces) if first else (parts,)
    in_specs = [pl.BlockSpec(memory_space=pltpu.SMEM)] * 3 + [in_vmem] * len(pieces) if first else [in_vmem]
    out_shape = [jax.ShapeDtypeStruct((SIDE * OWN // 2 + EXTRA, LO), jnp.int16)] * (SIDE - 1)
    out_shape.append(jax.ShapeDtypeStruct((SIDE, RANK, OWN // 2), jnp.float32))
    scratch = []
    if first:
        out_shape.append(jax.ShapeDtypeStruct((2 * RANK, TILES), jnp.bfloat16))
        scratch = [pltpu.VMEM((PEERS * ROWS, RANK), jnp.float32)] * 2 + [pltpu.VMEM((TILES, RANK), jnp.float32)]
    return pl.pallas_call(
        functools.partial(product_body, along_x=along_x, sizes=sizes, me=me, at=at),
        in_specs=in_specs + [in_vmem] * (2 * PARTS),
        out_specs=[in_vmem] * len(out_shape),
        out_shape=out_shape,
        scratch_shapes=scratch,
        compiler_params=pltpu.CompilerParams(vmem_limit_bytes=24 * MIB),
        cost_estimate=pl.CostEstimate(flops=2 * 10**9, bytes_accessed=6 * 10**6, transcendentals=0),
        name="products",
        interpret=interpret,
    )(*operands, *highs, *lows)


def relay_body(own_ref, a_ref, b_ref, c_ref, *refs, along_x, at):
    outs, mine_ref, sum_ref = refs[: SIDE - 1], refs[SIDE - 1], refs[SIDE]
    width = OWN // 2
    for other in range(SIDE):
        total = own_ref[other]
        for ref in (a_ref, b_ref, c_ref):
            levels = ref[SIDE * width :, :].astype(jnp.int32).astype(jnp.float32)
            total = total + decode(ref, other * width, width // LO, levels[other : other + 1])
        sum_ref[other] = total
    y, x = place(at)
    for k in range(SIDE):
        total = sum_ref[((y if along_x else x) + k) % SIDE]
        if k:
            outs[k - 1][width:, :] = encode(total, outs[k - 1], 0).astype(jnp.int32).astype(jnp.int16)
        else:
            mine_ref[...] = total


def relayed(along_x, own, received, at=None, interpret=False):
    in_vmem = pl.BlockSpec(memory_space=pltpu.VMEM)
    return pl.pallas_call(
        functools.partial(relay_body, along_x=along_x, at=at),
        in_specs=[in_vmem] * SIDE,
        out_specs=[in_vmem] * SIDE,
        out_shape=[jax.ShapeDtypeStruct((OWN // 2 + EXTRA, LO), jnp.int16)] * (SIDE - 1)
        + [jax.ShapeDtypeStruct((RANK, OWN // 2), jnp.float32)],
        scratch_shapes=[pltpu.VMEM((SIDE, RANK, OWN // 2), jnp.float32)],
        compiler_params=pltpu.CompilerParams(vmem_limit_bytes=20 * MIB),
        cost_estimate=pl.CostEstimate(flops=10**8, bytes_accessed=10**6, transcendentals=0),
        name="relayed",
        interpret=interpret,
    )(own, *received)


def finish_body(*refs):
    inverse_ref, out_ref = refs[2 * SIDE :]
    width = OWN // 2
    sums = []
    for own_ref, *received in (refs[:SIDE], refs[SIDE : 2 * SIDE]):
        total = own_ref[...]
        for ref in received:
            levels = ref[width:, :].astype(jnp.int32).astype(jnp.float32)
            total = total + decode(ref, 0, width // LO, levels[:1])
        sums.append(total)
    out_ref[...] = lax.dot_general(
        jnp.concatenate(sums, axis=1),
        inverse_ref[...],
        TN,
        precision=lax.Precision.HIGHEST,
        preferred_element_type=jnp.float32,
    )


def finish(first, second, inverse, interpret=False):
    in_vmem = pl.BlockSpec(memory_space=pltpu.VMEM)
    return pl.pallas_call(
        finish_body,
        in_specs=[in_vmem] * (2 * SIDE + 1),
        out_specs=in_vmem,
        out_shape=jax.ShapeDtypeStruct((OWN, RANK), jnp.float32),
        compiler_params=pltpu.CompilerParams(vmem_limit_bytes=20 * MIB),
        name="finish",
        interpret=interpret,
    )(*first, *second, inverse)


def gram_body(*refs, me):
    pieces, out_ref, gram_ref = refs[:-2], refs[-2], refs[-1]
    mine = (lax.axis_index("rows") if me is None else me) % SLICES
    for i in range(2):
        x = jnp.concatenate(
            [ref[at : at + ROWS, :] for ref in pieces for at in range(i * ROWS, ref.shape[0], 2 * ROWS)], axis=0
        )
        gram_ref[...] = lax.dot_general(x, x, TN, preferred_element_type=jnp.float32)
        out_ref[i] = gram_ref[pl.ds(pl.multiple_of(mine * SLICE, SLICE), SLICE), :]


def partial_grams(pieces, me=None, interpret=False):
    return pl.pallas_call(
        functools.partial(gram_body, me=me),
        in_specs=[pl.BlockSpec(memory_space=pltpu.VMEM)] * len(pieces),
        out_specs=pl.BlockSpec(memory_space=pltpu.VMEM),
        out_shape=jax.ShapeDtypeStruct((2, SLICE, RANK), jnp.float32),
        scratch_shapes=[pltpu.VMEM((RANK, RANK), jnp.float32)],
        compiler_params=pltpu.CompilerParams(vmem_limit_bytes=20 * MIB),
        cost_estimate=pl.CostEstimate(flops=10**9, bytes_accessed=3 * 10**6, transcendentals=0),
        name="partial_grams",
        interpret=interpret,
    )(*pieces)


def fold_body(after_ref, a_ref, b_ref, out_ref, *, multiply):
    del after_ref
    if multiply:
        out_ref[...] = (a_ref[0] + b_ref[0]) * (a_ref[1] + b_ref[1])
    else:
        out_ref[...] = a_ref[...] + b_ref[...]


def folded(after, a, b, multiply=False, interpret=False):
    in_vmem = pl.BlockSpec(memory_space=pltpu.VMEM)
    return pl.pallas_call(
        functools.partial(fold_body, multiply=multiply),
        in_specs=[pl.BlockSpec(memory_space=pl.ANY), in_vmem, in_vmem],
        out_specs=in_vmem,
        out_shape=jax.ShapeDtypeStruct(a.shape[1:] if multiply else a.shape, jnp.float32),
        compiler_params=pltpu.CompilerParams(vmem_limit_bytes=20 * MIB),
        name="folded",
        interpret=interpret,
    )(after, a, b)


def inverse_body(mine_ref, other_ref, out_ref, gram_ref, *, me):
    core = (lax.axis_index("rows") if me is None else me) % 2
    gram_ref[pl.ds(pl.multiple_of(core * SLICE, SLICE), SLICE), :] = mine_ref[...]
    gram_ref[pl.ds(pl.multiple_of((1 - core) * SLICE, SLICE), SLICE), :] = other_ref[...]
    a = gram_ref[...]
    lane = lax.broadcasted_iota(jnp.int32, (1, RANK), 1)
    sublane = lax.broadcasted_iota(jnp.int32, (RANK, 1), 0)
    for k in range(0, RANK, PIVOTS):
        order = range(PIVOTS)
        rows = [a[k + i : k + i + 1, :] for i in order]
        block = [[jnp.broadcast_to(rows[i][:, k + j : k + j + 1], (1, RANK)) for j in order] for i in order]
        columns = [a[:, k + i : k + i + 1] for i in order]
        inside = (lane >= k) & (lane < k + PIVOTS)
        rows = [jnp.where(inside, jnp.where(lane == k + i, 1.0, 0.0), rows[i]) for i in order]
        for j in order:
            scale = 1.0 / block[j][j]
            for i in order:
                if i != j:
                    ratio = block[i][j] * scale
                    rows[i] = rows[i] - ratio * rows[j]
                    for n in range(j + 1, PIVOTS):
                        block[i][n] = block[i][n] - ratio * block[j][n]
            rows[j] = rows[j] * scale
            for n in range(j + 1, PIVOTS):
                block[j][n] = block[j][n] * scale
        a = jnp.where(inside, 0.0, a)
        for i in order:
            a = a - columns[i] * rows[i]
        for i in order:
            a = jnp.where(sublane == k + i, rows[i], a)
    out_ref[...] = a


def inverted(mine, other, me=None, interpret=False):
    in_vmem = pl.BlockSpec(memory_space=pltpu.VMEM)
    return pl.pallas_call(
        functools.partial(inverse_body, me=me),
        in_specs=[in_vmem, in_vmem],
        out_specs=in_vmem,
        out_shape=jax.ShapeDtypeStruct((RANK, RANK), jnp.float32),
        scratch_shapes=[pltpu.VMEM((RANK, RANK), jnp.float32)],
        compiler_params=pltpu.CompilerParams(vmem_limit_bytes=20 * MIB),
        cost_estimate=pl.CostEstimate(flops=4 * 10**9, bytes_accessed=15 * 10**6, transcendentals=0),
        name="inverted",
        interpret=interpret,
    )(mine, other)


def swapped(bits):
    return [(i, i ^ bits) for i in range(PEERS)]


def along(xs, along_x):
    def moved(k):
        dy, dx = (0, k) if along_x else (k, 0)
        return [(SIDE * y + x, SIDE * ((y + dy) % SIDE) + (x + dx) % SIDE) for y in range(SIDE) for x in range(SIDE)]

    last, first, second = (lax.ppermute(xs[k - 1], "cols", moved(k)) for k in (2, 1, 3))
    return [first, last, second]


def on_device(values, tile_users, tile_items, tile_words, tile_count, factor_items, factor_words):
    across = swapped(1)
    around = [(2 * z, 2 * ((z + 1) % 8)) for z in range(8)] + [(2 * z + 1, 2 * ((z + 7) % 8) + 1) for z in range(8)]
    after = lax.optimization_barrier
    others = [lax.ppermute(x, "rows", across) for x in (factor_items, factor_words)]
    found = [jnp.concatenate([factor_items, factor_words, *others], axis=0)]
    highs, lows = [], []
    for step in range(4):
        arriving = lax.ppermute(found[-1] if step < 3 else found[-1][: 2 * ROWS], "rows", around)
        grams = folded(found[-1], grams, more) if step else partial_grams(found)
        more = lax.ppermute(grams, "cols", swapped(1 << step))
        high, low = build_weights(values, tile_users, step, found[-1])
        arriving, low, more = after((arriving, low, more))
        highs.append(high)
        lows.append(low)
        found.append(arriving)
    grams = folded(low, grams, more)
    more = lax.ppermute(grams, "rows", swapped(2))
    pieces = found + [lax.ppermute(x, "rows", across) for x in found[1:]]
    *pieces, more = after((*pieces, more))
    scalars = (tile_items, tile_words, tile_count)
    *out, own_a, parts = products(True, highs, lows, pieces=pieces, scalars=scalars)
    in_a = along(out, True)
    *out, own_b = products(False, highs, lows, parts=parts)
    in_b = along(out, False)
    grams = folded(own_b, grams, more)
    more = lax.ppermute(grams, "rows", swapped(4))
    *in_a, more = after((*in_a, more))
    *out, own_a = relayed(True, own_a, in_a)
    end_a = along(out, False)
    grams = folded(own_a, grams, more)
    more = lax.ppermute(grams, "rows", swapped(8))
    tied = after((*in_b, *end_a))
    in_b, end_a = tied[: SIDE - 1], tied[SIDE - 1 :]
    *out, own_b = relayed(False, own_b, in_b)
    end_b = along(out, True)
    grams = folded(own_b, grams, more, multiply=True)
    inverse = inverted(grams, lax.ppermute(grams, "rows", across))
    return finish((own_a, *end_a), (own_b, *end_b), inverse)


def solution(mesh):
    placed = (
        P(("rows", "cols"), None),
        P(("rows", "cols"), None),
        P(("rows", "cols")),
        P(("rows", "cols")),
        P(("rows", "cols")),
        P(("rows", "cols"), None),
        P(("rows", "cols"), None),
    )
    return jax.shard_map(
        on_device, mesh=mesh, in_specs=placed, out_specs=P(("rows", "cols"), None), check_vma=False
    )
```

```python
import functools

import jax
import jax.numpy as jnp
from jax import lax
from jax.experimental import pallas as pl
from jax.experimental.pallas import tpu as pltpu
from jax.sharding import PartitionSpec as P

RANK = 128
FIBER = 128
TILES = 512
ROWS = 256
OWN = 512
PEERS = 16
USERS = OWN * PEERS
LO = 128
HI = USERS // LO
EXTRA = 16
PARTS = 4
SLICES = 2
PIVOTS = 8
SLICE = RANK // SLICES
SIDE = 4
TILES_OWN = OWN // LO
PART = TILES // PARTS
STEP = 128.0
TOP = 32767.0
NT = (((1,), (1,)), ((), ()))
TN = (((0,), (0,)), ((), ()))
MIB = 1024 * 1024


def in_hbm(shape, dtype, interpret):
    return jax.ShapeDtypeStruct(shape, dtype) if interpret else pltpu.HBM(shape, dtype)


def build_body(v_ref, u_ref, after_ref, high_ref, low_ref, acc_ref, *, block):
    del after_ref
    pitch = block + 1
    hi_iota = lax.broadcasted_iota(jnp.int32, (HI, FIBER), 0)
    lo_iota = lax.broadcasted_iota(jnp.int32, (LO, FIBER), 0)

    def add_block(g, carry):
        at = pl.multiple_of(g * block, block)
        for k in range(block):
            v = v_ref[pl.ds(at + k, 1), :]
            u = u_ref[pl.ds(at + k, 1), :]
            vh = v.astype(jnp.bfloat16).astype(jnp.float32)
            vl = v - vh
            hit = hi_iota == (u >> 7)
            left = jnp.concatenate(
                [jnp.where(hit, vh, 0.0).astype(jnp.bfloat16), jnp.where(hit, vl, 0.0).astype(jnp.bfloat16)], axis=1
            )
            one = jnp.where(lo_iota == (u & 127), 1.0, 0.0).astype(jnp.bfloat16)
            right = jnp.concatenate([one, one], axis=1)
            acc_ref[pl.ds(k, HI, stride=pitch), :] = lax.dot_general(
                left, right, NT, preferred_element_type=jnp.float32
            )
        for h in range(HI):
            weight = acc_ref[pl.ds(h * pitch, block), :]
            high = weight.astype(jnp.bfloat16)
            high_ref[h, pl.ds(at, block), :] = high
            low_ref[h, pl.ds(at, block), :] = (weight - high.astype(jnp.float32)).astype(jnp.bfloat16)
        return carry

    lax.fori_loop(0, PART // block, add_block, 0)


def build_weights(values, users, part, after, block=32, interpret=False):
    return pl.pallas_call(
        functools.partial(build_body, block=block),
        grid=(1,),
        in_specs=[pl.BlockSpec((PART, FIBER), lambda i: (part, 0))] * 2 + [pl.BlockSpec(memory_space=pl.ANY)],
        out_specs=[pl.BlockSpec(memory_space=pltpu.VMEM)] * 2,
        out_shape=[pltpu.VMEM((HI, PART, LO), jnp.bfloat16)] * 2 if not interpret else [jax.ShapeDtypeStruct((HI, PART, LO), jnp.bfloat16)] * 2,
        scratch_shapes=[pltpu.VMEM((HI * (block + 1), LO), jnp.float32)],
        compiler_params=pltpu.CompilerParams(vmem_limit_bytes=20 * MIB),
        cost_estimate=pl.CostEstimate(flops=6 * 10**9, bytes_accessed=20 * 10**6, transcendentals=0),
        name="build_weights",
        interpret=interpret,
    )(values, users, after)


def sources(me):
    z, c = me // 2, me % 2
    way = 1 - 2 * c
    blocks = [(z, c), (z, 1 - c)]
    for k in range(1, 4):
        blocks += [(z - k * way, c), (z - k * way, 1 - c)]
    blocks.append((z - 4 * way, c))
    for k in range(1, 4):
        blocks += [(z + k * way, 1 - c), (z + k * way, c)]
    blocks.append((z + 4 * way, 1 - c))
    return [(chip + 8) % 8 * 2 + core for chip, core in blocks]


def encode(total, store, base):
    most = jnp.max(jnp.abs(total), axis=1, keepdims=True)
    level = jnp.ceil(jnp.log2(jnp.maximum(most, 1e-35)) * STEP + 1.0)
    coded = jnp.round(total * jnp.exp2(level * (-1.0 / STEP)) * TOP).astype(jnp.int32).astype(jnp.int16)
    for i in range(total.shape[1] // LO):
        store[base + i * RANK : base + (i + 1) * RANK, :] = coded[:, i * LO : (i + 1) * LO]
    return jnp.broadcast_to(level, (RANK, RANK)).T[:EXTRA]


def decode(ref, base, tiles, levels):
    level = jnp.broadcast_to(levels, (RANK, RANK)).T
    scale = jnp.exp2(level * (1.0 / STEP)) * (1.0 / TOP)
    return jnp.concatenate(
        [
            ref[base + i * RANK : base + (i + 1) * RANK, :].astype(jnp.int32).astype(jnp.float32) * scale
            for i in range(tiles)
        ],
        axis=1,
    )


def place(me):
    at = lax.axis_index("cols") if me is None else me
    return at // SIDE, at % SIDE


def product_body(*refs, along_x, sizes, me, at):
    first = sizes is not None
    if first:
        item_at, word_at, count = refs[:3]
        pieces = refs[3 : 3 + len(sizes)]
        refs = refs[3 + len(sizes) :]
    else:
        parts_ref, refs = refs[0], refs[1:]
    weights, refs = refs[: 2 * PARTS], refs[2 * PARTS :]
    outs, own_ref = refs[: SIDE - 1], refs[SIDE - 1]
    if first:
        parts_ref, item_ref, word_ref, khatri_ref = refs[SIDE:]
        source = iter(sources(lax.axis_index("rows") if me is None else me))
        for ref, size in zip(pieces, sizes, strict=True):
            for j in range(size):
                row = pl.multiple_of(next(source) * ROWS, ROWS)
                item_ref[pl.ds(row, ROWS), :] = ref[2 * j * ROWS : (2 * j + 1) * ROWS, :].astype(jnp.float32)
                word_ref[pl.ds(row, ROWS), :] = ref[(2 * j + 1) * ROWS : (2 * j + 2) * ROWS, :].astype(jnp.float32)

        def take(g, carry):
            for k in range(16):
                t = g * 16 + k
                khatri_ref[pl.ds(t, 1), :] = item_ref[pl.ds(item_at[t], 1), :] * word_ref[pl.ds(word_at[t], 1), :]
            return carry

        lax.fori_loop(0, TILES // 16, take, 0)
        live = lax.broadcasted_iota(jnp.int32, (TILES, RANK), 0) < count[0]
        khatri = jnp.where(live, khatri_ref[...], 0.0).T
        high = khatri.astype(jnp.bfloat16)
        parts_ref[:RANK, :] = high
        parts_ref[RANK:, :] = (khatri - high.astype(jnp.float32)).astype(jnp.bfloat16)

    y, x = place(at)
    half = 0 if along_x else TILES_OWN // 2
    for k in (1, 2, 3, 0):
        rows = []
        for other in range(SIDE):
            owner = other * SIDE + (x + k) % SIDE if along_x else (y + k) % SIDE * SIDE + other
            base = owner * TILES_OWN + half

            def joined(refs, base=base):
                return jnp.concatenate(
                    [jnp.concatenate([ref[base + i] for ref in refs], axis=0) for i in range(TILES_OWN // 2)], axis=1
                )

            both = jnp.dot(parts_ref[...], joined(weights[:PARTS]), preferred_element_type=jnp.float32)
            rest = jnp.dot(parts_ref[:RANK, :], joined(weights[PARTS:]), preferred_element_type=jnp.float32)
            total = both[:RANK] + (both[RANK:] + rest)
            if k:
                rows.append(encode(total, outs[k - 1], other * (OWN // 2)))
            else:
                own_ref[other] = total
        if k:
            levels = jnp.concatenate([row[:1] for row in rows] + [rows[0][: EXTRA - SIDE]], axis=0)
            outs[k - 1][SIDE * OWN // 2 :, :] = levels.astype(jnp.int32).astype(jnp.int16)


def products(along_x, highs, lows, *, parts=None, pieces=None, scalars=None, me=None, at=None, interpret=False):
    if not interpret:
        highs = [pltpu.with_memory_space_constraint(x, pltpu.VMEM) for x in highs]
        lows = [pltpu.with_memory_space_constraint(x, pltpu.VMEM) for x in lows]
    in_vmem = pl.BlockSpec(memory_space=pltpu.VMEM)
    first = parts is None
    sizes = [x.shape[0] // (2 * ROWS) for x in pieces] if first else None
    operands = (*scalars, *pieces) if first else (parts,)
    in_specs = [pl.BlockSpec(memory_space=pltpu.SMEM)] * 3 + [in_vmem] * len(pieces) if first else [in_vmem]
    out_shape = [jax.ShapeDtypeStruct((SIDE * OWN // 2 + EXTRA, LO), jnp.int16)] * (SIDE - 1)
    out_shape.append(jax.ShapeDtypeStruct((SIDE, RANK, OWN // 2), jnp.float32))
    scratch = []
    if first:
        out_shape.append(jax.ShapeDtypeStruct((2 * RANK, TILES), jnp.bfloat16))
        scratch = [pltpu.VMEM((PEERS * ROWS, RANK), jnp.float32)] * 2 + [pltpu.VMEM((TILES, RANK), jnp.float32)]
    return pl.pallas_call(
        functools.partial(product_body, along_x=along_x, sizes=sizes, me=me, at=at),
        in_specs=in_specs + [in_vmem] * (2 * PARTS),
        out_specs=[in_vmem] * len(out_shape),
        out_shape=out_shape,
        scratch_shapes=scratch,
        compiler_params=pltpu.CompilerParams(vmem_limit_bytes=24 * MIB),
        cost_estimate=pl.CostEstimate(flops=4 * 10**9, bytes_accessed=13 * 10**6, transcendentals=0),
        name="products",
        interpret=interpret,
    )(*operands, *highs, *lows)


def relay_body(own_ref, a_ref, b_ref, c_ref, *refs, along_x, at):
    outs, mine_ref, sum_ref = refs[: SIDE - 1], refs[SIDE - 1], refs[SIDE]
    width = OWN // 2
    for other in range(SIDE):
        total = own_ref[other]
        for ref in (a_ref, b_ref, c_ref):
            levels = ref[SIDE * width :, :].astype(jnp.int32).astype(jnp.float32)
            total = total + decode(ref, other * width, width // LO, levels[other : other + 1])
        sum_ref[other] = total
    y, x = place(at)
    for k in range(SIDE):
        total = sum_ref[((y if along_x else x) + k) % SIDE]
        if k:
            outs[k - 1][width:, :] = encode(total, outs[k - 1], 0).astype(jnp.int32).astype(jnp.int16)
        else:
            mine_ref[...] = total


def relayed(along_x, own, received, at=None, interpret=False):
    in_vmem = pl.BlockSpec(memory_space=pltpu.VMEM)
    return pl.pallas_call(
        functools.partial(relay_body, along_x=along_x, at=at),
        in_specs=[in_vmem] * SIDE,
        out_specs=[in_vmem] * SIDE,
        out_shape=[jax.ShapeDtypeStruct((OWN // 2 + EXTRA, LO), jnp.int16)] * (SIDE - 1)
        + [jax.ShapeDtypeStruct((RANK, OWN // 2), jnp.float32)],
        scratch_shapes=[pltpu.VMEM((SIDE, RANK, OWN // 2), jnp.float32)],
        compiler_params=pltpu.CompilerParams(vmem_limit_bytes=20 * MIB),
        cost_estimate=pl.CostEstimate(flops=2 * 10**9, bytes_accessed=7 * 10**6, transcendentals=0),
        name="relayed",
        interpret=interpret,
    )(own, *received)


def finish_body(*refs):
    inverse_ref, out_ref = refs[2 * SIDE :]
    width = OWN // 2
    sums = []
    for own_ref, *received in (refs[:SIDE], refs[SIDE : 2 * SIDE]):
        total = own_ref[...]
        for ref in received:
            levels = ref[width:, :].astype(jnp.int32).astype(jnp.float32)
            total = total + decode(ref, 0, width // LO, levels[:1])
        sums.append(total)
    out_ref[...] = lax.dot_general(
        jnp.concatenate(sums, axis=1),
        inverse_ref[...],
        TN,
        precision=lax.Precision.HIGHEST,
        preferred_element_type=jnp.float32,
    )


def finish(first, second, inverse, interpret=False):
    in_vmem = pl.BlockSpec(memory_space=pltpu.VMEM)
    return pl.pallas_call(
        finish_body,
        in_specs=[in_vmem] * (2 * SIDE + 1),
        out_specs=in_vmem,
        out_shape=jax.ShapeDtypeStruct((OWN, RANK), jnp.float32),
        compiler_params=pltpu.CompilerParams(vmem_limit_bytes=20 * MIB),
        name="finish",
        interpret=interpret,
    )(*first, *second, inverse)


def gram_body(*refs, me):
    pieces, out_ref, gram_ref = refs[:-2], refs[-2], refs[-1]
    mine = (lax.axis_index("rows") if me is None else me) % SLICES
    for i in range(2):
        x = jnp.concatenate(
            [ref[at : at + ROWS, :] for ref in pieces for at in range(i * ROWS, ref.shape[0], 2 * ROWS)], axis=0
        )
        gram_ref[...] = lax.dot_general(x, x, TN, preferred_element_type=jnp.float32)
        out_ref[i] = gram_ref[pl.ds(pl.multiple_of(mine * SLICE, SLICE), SLICE), :]


def partial_grams(pieces, me=None, interpret=False):
    return pl.pallas_call(
        functools.partial(gram_body, me=me),
        in_specs=[pl.BlockSpec(memory_space=pltpu.VMEM)] * len(pieces),
        out_specs=pl.BlockSpec(memory_space=pltpu.VMEM),
        out_shape=jax.ShapeDtypeStruct((2, SLICE, RANK), jnp.float32),
        scratch_shapes=[pltpu.VMEM((RANK, RANK), jnp.float32)],
        compiler_params=pltpu.CompilerParams(vmem_limit_bytes=20 * MIB),
        cost_estimate=pl.CostEstimate(flops=10**9, bytes_accessed=3 * 10**6, transcendentals=0),
        name="partial_grams",
        interpret=interpret,
    )(*pieces)


def fold_body(after_ref, a_ref, b_ref, out_ref, *, multiply):
    del after_ref
    if multiply:
        out_ref[...] = (a_ref[0] + b_ref[0]) * (a_ref[1] + b_ref[1])
    else:
        out_ref[...] = a_ref[...] + b_ref[...]


def folded(after, a, b, multiply=False, interpret=False):
    in_vmem = pl.BlockSpec(memory_space=pltpu.VMEM)
    return pl.pallas_call(
        functools.partial(fold_body, multiply=multiply),
        in_specs=[pl.BlockSpec(memory_space=pl.ANY), in_vmem, in_vmem],
        out_specs=in_vmem,
        out_shape=jax.ShapeDtypeStruct(a.shape[1:] if multiply else a.shape, jnp.float32),
        compiler_params=pltpu.CompilerParams(vmem_limit_bytes=20 * MIB),
        name="folded",
        interpret=interpret,
    )(after, a, b)


def inverse_body(mine_ref, other_ref, out_ref, gram_ref, *, me):
    core = (lax.axis_index("rows") if me is None else me) % 2
    gram_ref[pl.ds(pl.multiple_of(core * SLICE, SLICE), SLICE), :] = mine_ref[...]
    gram_ref[pl.ds(pl.multiple_of((1 - core) * SLICE, SLICE), SLICE), :] = other_ref[...]
    a = gram_ref[...]
    lane = lax.broadcasted_iota(jnp.int32, (1, RANK), 1)
    sublane = lax.broadcasted_iota(jnp.int32, (RANK, 1), 0)
    for k in range(0, RANK, PIVOTS):
        order = range(PIVOTS)
        rows = [a[k + i : k + i + 1, :] for i in order]
        block = [[jnp.broadcast_to(rows[i][:, k + j : k + j + 1], (1, RANK)) for j in order] for i in order]
        columns = [a[:, k + i : k + i + 1] for i in order]
        inside = (lane >= k) & (lane < k + PIVOTS)
        rows = [jnp.where(inside, jnp.where(lane == k + i, 1.0, 0.0), rows[i]) for i in order]
        for j in order:
            scale = 1.0 / block[j][j]
            for i in order:
                if i != j:
                    ratio = block[i][j] * scale
                    rows[i] = rows[i] - ratio * rows[j]
                    for n in range(j + 1, PIVOTS):
                        block[i][n] = block[i][n] - ratio * block[j][n]
            rows[j] = rows[j] * scale
            for n in range(j + 1, PIVOTS):
                block[j][n] = block[j][n] * scale
        a = jnp.where(inside, 0.0, a)
        for i in order:
            a = a - columns[i] * rows[i]
        for i in order:
            a = jnp.where(sublane == k + i, rows[i], a)
    out_ref[...] = a


def inverted(mine, other, me=None, interpret=False):
    in_vmem = pl.BlockSpec(memory_space=pltpu.VMEM)
    return pl.pallas_call(
        functools.partial(inverse_body, me=me),
        in_specs=[in_vmem, in_vmem],
        out_specs=in_vmem,
        out_shape=jax.ShapeDtypeStruct((RANK, RANK), jnp.float32),
        scratch_shapes=[pltpu.VMEM((RANK, RANK), jnp.float32)],
        compiler_params=pltpu.CompilerParams(vmem_limit_bytes=20 * MIB),
        cost_estimate=pl.CostEstimate(flops=4 * 10**9, bytes_accessed=15 * 10**6, transcendentals=0),
        name="inverted",
        interpret=interpret,
    )(mine, other)


def swapped(bits):
    return [(i, i ^ bits) for i in range(PEERS)]


def along(xs, along_x):
    def moved(k):
        dy, dx = (0, k) if along_x else (k, 0)
        return [(SIDE * y + x, SIDE * ((y + dy) % SIDE) + (x + dx) % SIDE) for y in range(SIDE) for x in range(SIDE)]

    last, first, second = (lax.ppermute(xs[k - 1], "cols", moved(k)) for k in (2, 1, 3))
    return [first, last, second]


def on_device(values, tile_users, tile_items, tile_words, tile_count, factor_items, factor_words):
    across = swapped(1)
    around = [(2 * z, 2 * ((z + 1) % 8)) for z in range(8)] + [(2 * z + 1, 2 * ((z + 7) % 8) + 1) for z in range(8)]
    after = lax.optimization_barrier
    others = [lax.ppermute(x, "rows", across) for x in (factor_items, factor_words)]
    found = [jnp.concatenate([factor_items, factor_words, *others], axis=0)]
    highs, lows = [], []
    grams = partial_grams(found)
    more = lax.ppermute(grams, "cols", swapped(1))
    for step in range(4):
        arriving = lax.ppermute(found[-1] if step < 3 else found[-1][: 2 * ROWS], "rows", around)
        high, low = build_weights(values, tile_users, step, found[-1])
        if step == 0:
            grams = folded(found[-1], grams, more)
            arriving, low, grams = after((arriving, low, grams))
            more = lax.ppermute(grams, "cols", swapped(2))
        else:
            grams = folded(low if step == 1 else found[-1], grams, more)
            more = lax.ppermute(grams, *(("cols", swapped(2 << step)) if step < 3 else ("rows", swapped(2))))
            if step == 1:
                arriving, low = after((arriving, low))
            else:
                arriving, low, more = after((arriving, low, more))
        highs.append(high)
        lows.append(low)
        found.append(arriving)
    pieces = found + [lax.ppermute(x, "rows", across) for x in found[1:]]
    scalars = (tile_items, tile_words, tile_count)
    *out, own_a, parts = products(True, highs, lows, pieces=pieces, scalars=scalars)
    in_a = along(out, True)
    *out, own_b = products(False, highs, lows, parts=parts)
    in_b = along(out, False)
    grams = folded(own_b, grams, more)
    more = lax.ppermute(grams, "rows", swapped(4))
    own_a, more = after((own_a, more))
    *out, own_a = relayed(True, own_a, in_a)
    end_a = along(out, False)
    grams = folded(own_a, grams, more)
    more = lax.ppermute(grams, "rows", swapped(8))
    *out, own_b = relayed(False, own_b, in_b)
    end_b = along(out, True)
    grams = folded(own_b, grams, more, multiply=True)
    inverse = inverted(grams, lax.ppermute(grams, "rows", across))
    return finish((own_a, *end_a), (own_b, *end_b), inverse)


def solution(mesh):
    placed = (
        P(("rows", "cols"), None),
        P(("rows", "cols"), None),
        P(("rows", "cols")),
        P(("rows", "cols")),
        P(("rows", "cols")),
        P(("rows", "cols"), None),
        P(("rows", "cols"), None),
    )
    return jax.shard_map(
        on_device, mesh=mesh, in_specs=placed, out_specs=P(("rows", "cols"), None), check_vma=False
    )
```

```python
import functools

import jax
import jax.numpy as jnp
from jax import lax
from jax.experimental import pallas as pl
from jax.experimental.pallas import tpu as pltpu
from jax.sharding import PartitionSpec as P

RANK = 128
FIBER = 128
TILES = 512
ROWS = 256
OWN = 512
PEERS = 16
USERS = OWN * PEERS
LO = 128
HI = USERS // LO
EXTRA = 16
PARTS = 4
SLICES = 2
PIVOTS = 8
SLICE = RANK // SLICES
SIDE = 4
TILES_OWN = OWN // LO
PART = TILES // PARTS
STEP = 128.0
TOP = 32767.0
NT = (((1,), (1,)), ((), ()))
TN = (((0,), (0,)), ((), ()))
MIB = 1024 * 1024


def in_hbm(shape, dtype, interpret):
    return jax.ShapeDtypeStruct(shape, dtype) if interpret else pltpu.HBM(shape, dtype)


def build_body(v_ref, u_ref, after_ref, high_ref, low_ref, acc_ref, *, block):
    del after_ref
    pitch = block + 1
    narrow = jnp.bfloat16
    hi_iota = lax.broadcasted_iota(jnp.int32, (HI, FIBER), 0).astype(narrow)
    lo_iota = lax.broadcasted_iota(jnp.int32, (LO, FIBER), 0).astype(narrow)
    zero = jnp.zeros((HI, FIBER), narrow)

    def spread(row, rows):
        return jnp.concatenate([jnp.broadcast_to(row, (16, FIBER)).astype(narrow)] * (rows // 16), axis=0)

    def hits(t):
        v = v_ref[pl.ds(t, 1), :]
        u = u_ref[pl.ds(t, 1), :]
        vh = v.astype(narrow).astype(jnp.float32)
        hit = hi_iota == spread((u >> 7).astype(jnp.float32), HI)
        low = lo_iota == spread((u & 127).astype(jnp.float32), LO)
        one = jnp.where(low, jnp.ones((LO, FIBER), narrow), jnp.zeros((LO, FIBER), narrow))
        return jnp.where(hit, spread(vh, HI), zero), jnp.where(hit, spread(v - vh, HI), zero), one

    def add_block(g, carry):
        at = pl.multiple_of(g * block, block)
        for k in range(0, block, 2):
            a, a_low, a_one = hits(at + k)
            b, b_low, b_one = hits(at + k + 1)
            rows = [(a, zero), (a_low, zero), (zero, b), (zero, b_low)]
            left = jnp.concatenate([jnp.concatenate(row, axis=1) for row in rows], axis=0)
            right = jnp.concatenate([a_one, b_one], axis=1)
            both = lax.dot_general(left, right, NT, preferred_element_type=jnp.float32)
            acc_ref[pl.ds(k, HI, stride=pitch), :] = both[:HI] + both[HI : 2 * HI]
            acc_ref[pl.ds(k + 1, HI, stride=pitch), :] = both[2 * HI : 3 * HI] + both[3 * HI :]
        for h in range(HI):
            weight = acc_ref[pl.ds(h * pitch, block), :]
            high = weight.astype(jnp.bfloat16)
            high_ref[h, pl.ds(at, block), :] = high
            low_ref[h, pl.ds(at, block), :] = (weight - high.astype(jnp.float32)).astype(jnp.bfloat16)
        return carry

    lax.fori_loop(0, PART // block, add_block, 0)


def build_weights(values, users, part, after, block=32, interpret=False):
    return pl.pallas_call(
        functools.partial(build_body, block=block),
        grid=(1,),
        in_specs=[pl.BlockSpec((PART, FIBER), lambda i: (part, 0))] * 2 + [pl.BlockSpec(memory_space=pl.ANY)],
        out_specs=[pl.BlockSpec(memory_space=pltpu.VMEM)] * 2,
        out_shape=[pltpu.VMEM((HI, PART, LO), jnp.bfloat16)] * 2 if not interpret else [jax.ShapeDtypeStruct((HI, PART, LO), jnp.bfloat16)] * 2,
        scratch_shapes=[pltpu.VMEM((HI * (block + 1), LO), jnp.float32)],
        compiler_params=pltpu.CompilerParams(vmem_limit_bytes=20 * MIB),
        cost_estimate=pl.CostEstimate(flops=6 * 10**9, bytes_accessed=20 * 10**6, transcendentals=0),
        name="build_weights",
        interpret=interpret,
    )(values, users, after)


def sources(me):
    z, c = me // 2, me % 2
    way = 1 - 2 * c
    blocks = [(z, c), (z, 1 - c)]
    for k in range(1, 4):
        blocks += [(z - k * way, c), (z - k * way, 1 - c)]
    blocks.append((z - 4 * way, c))
    for k in range(1, 4):
        blocks += [(z + k * way, 1 - c), (z + k * way, c)]
    blocks.append((z + 4 * way, 1 - c))
    return [(chip + 8) % 8 * 2 + core for chip, core in blocks]


def encode(total, store, base):
    most = jnp.max(jnp.abs(total), axis=1, keepdims=True)
    level = jnp.ceil(jnp.log2(jnp.maximum(most, 1e-35)) * STEP + 1.0)
    coded = jnp.round(total * jnp.exp2(level * (-1.0 / STEP)) * TOP).astype(jnp.int32).astype(jnp.int16)
    for i in range(total.shape[1] // LO):
        store[base + i * RANK : base + (i + 1) * RANK, :] = coded[:, i * LO : (i + 1) * LO]
    return jnp.broadcast_to(level, (RANK, RANK)).T[:EXTRA]


def decode(ref, base, tiles, levels):
    level = jnp.broadcast_to(levels, (RANK, RANK)).T
    scale = jnp.exp2(level * (1.0 / STEP)) * (1.0 / TOP)
    return jnp.concatenate(
        [
            ref[base + i * RANK : base + (i + 1) * RANK, :].astype(jnp.int32).astype(jnp.float32) * scale
            for i in range(tiles)
        ],
        axis=1,
    )


def place(me):
    at = lax.axis_index("cols") if me is None else me
    return at // SIDE, at % SIDE


def product_body(*refs, along_x, sizes, me, at):
    first = sizes is not None
    if first:
        item_at, word_at, count = refs[:3]
        pieces = refs[3 : 3 + len(sizes)]
        refs = refs[3 + len(sizes) :]
    else:
        parts_ref, refs = refs[0], refs[1:]
    weights, refs = refs[: 2 * PARTS], refs[2 * PARTS :]
    outs, own_ref = refs[: SIDE - 1], refs[SIDE - 1]
    if first:
        parts_ref, item_ref, word_ref, khatri_ref = refs[SIDE:]
        source = iter(sources(lax.axis_index("rows") if me is None else me))
        for ref, size in zip(pieces, sizes, strict=True):
            for j in range(size):
                row = pl.multiple_of(next(source) * ROWS, ROWS)
                item_ref[pl.ds(row, ROWS), :] = ref[2 * j * ROWS : (2 * j + 1) * ROWS, :].astype(jnp.float32)
                word_ref[pl.ds(row, ROWS), :] = ref[(2 * j + 1) * ROWS : (2 * j + 2) * ROWS, :].astype(jnp.float32)

        def take(g, carry):
            for k in range(16):
                t = g * 16 + k
                khatri_ref[pl.ds(t, 1), :] = item_ref[pl.ds(item_at[t], 1), :] * word_ref[pl.ds(word_at[t], 1), :]
            return carry

        lax.fori_loop(0, TILES // 16, take, 0)
        live = lax.broadcasted_iota(jnp.int32, (TILES, RANK), 0) < count[0]
        khatri = jnp.where(live, khatri_ref[...], 0.0).T
        high = khatri.astype(jnp.bfloat16)
        parts_ref[:RANK, :] = high
        parts_ref[RANK:, :] = (khatri - high.astype(jnp.float32)).astype(jnp.bfloat16)

    y, x = place(at)
    half = 0 if along_x else TILES_OWN // 2
    for k in (1, 2, 3, 0):
        rows = []
        for other in range(SIDE):
            owner = other * SIDE + (x + k) % SIDE if along_x else (y + k) % SIDE * SIDE + other
            base = owner * TILES_OWN + half

            def joined(refs, base=base):
                return jnp.concatenate(
                    [jnp.concatenate([ref[base + i] for ref in refs], axis=0) for i in range(TILES_OWN // 2)], axis=1
                )

            both = jnp.dot(parts_ref[...], joined(weights[:PARTS]), preferred_element_type=jnp.float32)
            rest = jnp.dot(parts_ref[:RANK, :], joined(weights[PARTS:]), preferred_element_type=jnp.float32)
            total = both[:RANK] + (both[RANK:] + rest)
            if k:
                rows.append(encode(total, outs[k - 1], other * (OWN // 2)))
            else:
                own_ref[other] = total
        if k:
            levels = jnp.concatenate([row[:1] for row in rows] + [rows[0][: EXTRA - SIDE]], axis=0)
            outs[k - 1][SIDE * OWN // 2 :, :] = levels.astype(jnp.int32).astype(jnp.int16)


def products(along_x, highs, lows, *, parts=None, pieces=None, scalars=None, me=None, at=None, interpret=False):
    if not interpret:
        highs = [pltpu.with_memory_space_constraint(x, pltpu.VMEM) for x in highs]
        lows = [pltpu.with_memory_space_constraint(x, pltpu.VMEM) for x in lows]
    in_vmem = pl.BlockSpec(memory_space=pltpu.VMEM)
    first = parts is None
    sizes = [x.shape[0] // (2 * ROWS) for x in pieces] if first else None
    operands = (*scalars, *pieces) if first else (parts,)
    in_specs = [pl.BlockSpec(memory_space=pltpu.SMEM)] * 3 + [in_vmem] * len(pieces) if first else [in_vmem]
    out_shape = [jax.ShapeDtypeStruct((SIDE * OWN // 2 + EXTRA, LO), jnp.int16)] * (SIDE - 1)
    out_shape.append(jax.ShapeDtypeStruct((SIDE, RANK, OWN // 2), jnp.float32))
    scratch = []
    if first:
        out_shape.append(jax.ShapeDtypeStruct((2 * RANK, TILES), jnp.bfloat16))
        scratch = [pltpu.VMEM((PEERS * ROWS, RANK), jnp.float32)] * 2 + [pltpu.VMEM((TILES, RANK), jnp.float32)]
    return pl.pallas_call(
        functools.partial(product_body, along_x=along_x, sizes=sizes, me=me, at=at),
        in_specs=in_specs + [in_vmem] * (2 * PARTS),
        out_specs=[in_vmem] * len(out_shape),
        out_shape=out_shape,
        scratch_shapes=scratch,
        compiler_params=pltpu.CompilerParams(vmem_limit_bytes=24 * MIB),
        cost_estimate=pl.CostEstimate(flops=4 * 10**9, bytes_accessed=13 * 10**6, transcendentals=0),
        name="products",
        interpret=interpret,
    )(*operands, *highs, *lows)


def relay_body(own_ref, a_ref, b_ref, c_ref, *refs, along_x, at):
    outs, mine_ref, sum_ref = refs[: SIDE - 1], refs[SIDE - 1], refs[SIDE]
    width = OWN // 2
    for other in range(SIDE):
        total = own_ref[other]
        for ref in (a_ref, b_ref, c_ref):
            levels = ref[SIDE * width :, :].astype(jnp.int32).astype(jnp.float32)
            total = total + decode(ref, other * width, width // LO, levels[other : other + 1])
        sum_ref[other] = total
    y, x = place(at)
    for k in range(SIDE):
        total = sum_ref[((y if along_x else x) + k) % SIDE]
        if k:
            outs[k - 1][width:, :] = encode(total, outs[k - 1], 0).astype(jnp.int32).astype(jnp.int16)
        else:
            mine_ref[...] = total


def relayed(along_x, own, received, at=None, interpret=False):
    in_vmem = pl.BlockSpec(memory_space=pltpu.VMEM)
    return pl.pallas_call(
        functools.partial(relay_body, along_x=along_x, at=at),
        in_specs=[in_vmem] * SIDE,
        out_specs=[in_vmem] * SIDE,
        out_shape=[jax.ShapeDtypeStruct((OWN // 2 + EXTRA, LO), jnp.int16)] * (SIDE - 1)
        + [jax.ShapeDtypeStruct((RANK, OWN // 2), jnp.float32)],
        scratch_shapes=[pltpu.VMEM((SIDE, RANK, OWN // 2), jnp.float32)],
        compiler_params=pltpu.CompilerParams(vmem_limit_bytes=20 * MIB),
        cost_estimate=pl.CostEstimate(flops=2 * 10**9, bytes_accessed=7 * 10**6, transcendentals=0),
        name="relayed",
        interpret=interpret,
    )(own, *received)


def finish_body(*refs):
    inverse_ref, out_ref = refs[2 * SIDE :]
    width = OWN // 2
    sums = []
    for own_ref, *received in (refs[:SIDE], refs[SIDE : 2 * SIDE]):
        total = own_ref[...]
        for ref in received:
            levels = ref[width:, :].astype(jnp.int32).astype(jnp.float32)
            total = total + decode(ref, 0, width // LO, levels[:1])
        sums.append(total)
    out_ref[...] = lax.dot_general(
        jnp.concatenate(sums, axis=1),
        inverse_ref[...],
        TN,
        precision=lax.Precision.HIGHEST,
        preferred_element_type=jnp.float32,
    )


def finish(first, second, inverse, interpret=False):
    in_vmem = pl.BlockSpec(memory_space=pltpu.VMEM)
    return pl.pallas_call(
        finish_body,
        in_specs=[in_vmem] * (2 * SIDE + 1),
        out_specs=in_vmem,
        out_shape=jax.ShapeDtypeStruct((OWN, RANK), jnp.float32),
        compiler_params=pltpu.CompilerParams(vmem_limit_bytes=20 * MIB),
        name="finish",
        interpret=interpret,
    )(*first, *second, inverse)


def gram_body(*refs, me):
    pieces, out_ref, gram_ref = refs[:-2], refs[-2], refs[-1]
    mine = (lax.axis_index("rows") if me is None else me) % SLICES
    for i in range(2):
        x = jnp.concatenate(
            [ref[at : at + ROWS, :] for ref in pieces for at in range(i * ROWS, ref.shape[0], 2 * ROWS)], axis=0
        )
        gram_ref[...] = lax.dot_general(x, x, TN, preferred_element_type=jnp.float32)
        out_ref[i] = gram_ref[pl.ds(pl.multiple_of(mine * SLICE, SLICE), SLICE), :]


def partial_grams(pieces, me=None, interpret=False):
    return pl.pallas_call(
        functools.partial(gram_body, me=me),
        in_specs=[pl.BlockSpec(memory_space=pltpu.VMEM)] * len(pieces),
        out_specs=pl.BlockSpec(memory_space=pltpu.VMEM),
        out_shape=jax.ShapeDtypeStruct((2, SLICE, RANK), jnp.float32),
        scratch_shapes=[pltpu.VMEM((RANK, RANK), jnp.float32)],
        compiler_params=pltpu.CompilerParams(vmem_limit_bytes=20 * MIB),
        cost_estimate=pl.CostEstimate(flops=10**9, bytes_accessed=3 * 10**6, transcendentals=0),
        name="partial_grams",
        interpret=interpret,
    )(*pieces)


def fold_body(after_ref, a_ref, b_ref, out_ref, *, multiply):
    del after_ref
    if multiply:
        out_ref[...] = (a_ref[0] + b_ref[0]) * (a_ref[1] + b_ref[1])
    else:
        out_ref[...] = a_ref[...] + b_ref[...]


def folded(after, a, b, multiply=False, interpret=False):
    in_vmem = pl.BlockSpec(memory_space=pltpu.VMEM)
    return pl.pallas_call(
        functools.partial(fold_body, multiply=multiply),
        in_specs=[pl.BlockSpec(memory_space=pl.ANY), in_vmem, in_vmem],
        out_specs=in_vmem,
        out_shape=jax.ShapeDtypeStruct(a.shape[1:] if multiply else a.shape, jnp.float32),
        compiler_params=pltpu.CompilerParams(vmem_limit_bytes=20 * MIB),
        name="folded",
        interpret=interpret,
    )(after, a, b)


def inverse_body(mine_ref, other_ref, out_ref, gram_ref, *, me):
    core = (lax.axis_index("rows") if me is None else me) % 2
    gram_ref[pl.ds(pl.multiple_of(core * SLICE, SLICE), SLICE), :] = mine_ref[...]
    gram_ref[pl.ds(pl.multiple_of((1 - core) * SLICE, SLICE), SLICE), :] = other_ref[...]
    a = gram_ref[...]
    lane = lax.broadcasted_iota(jnp.int32, (1, RANK), 1)
    sublane = lax.broadcasted_iota(jnp.int32, (RANK, 1), 0)
    for k in range(0, RANK, PIVOTS):
        order = range(PIVOTS)
        rows = [a[k + i : k + i + 1, :] for i in order]
        block = [[jnp.broadcast_to(rows[i][:, k + j : k + j + 1], (1, RANK)) for j in order] for i in order]
        columns = [a[:, k + i : k + i + 1] for i in order]
        inside = (lane >= k) & (lane < k + PIVOTS)
        rows = [jnp.where(inside, jnp.where(lane == k + i, 1.0, 0.0), rows[i]) for i in order]
        for j in order:
            scale = 1.0 / block[j][j]
            for i in order:
                if i != j:
                    ratio = block[i][j] * scale
                    rows[i] = rows[i] - ratio * rows[j]
                    for n in range(j + 1, PIVOTS):
                        block[i][n] = block[i][n] - ratio * block[j][n]
            rows[j] = rows[j] * scale
            for n in range(j + 1, PIVOTS):
                block[j][n] = block[j][n] * scale
        a = jnp.where(inside, 0.0, a)
        for i in order:
            a = a - columns[i] * rows[i]
        for i in order:
            a = jnp.where(sublane == k + i, rows[i], a)
    out_ref[...] = a


def inverted(mine, other, me=None, interpret=False):
    in_vmem = pl.BlockSpec(memory_space=pltpu.VMEM)
    return pl.pallas_call(
        functools.partial(inverse_body, me=me),
        in_specs=[in_vmem, in_vmem],
        out_specs=in_vmem,
        out_shape=jax.ShapeDtypeStruct((RANK, RANK), jnp.float32),
        scratch_shapes=[pltpu.VMEM((RANK, RANK), jnp.float32)],
        compiler_params=pltpu.CompilerParams(vmem_limit_bytes=20 * MIB),
        cost_estimate=pl.CostEstimate(flops=4 * 10**9, bytes_accessed=15 * 10**6, transcendentals=0),
        name="inverted",
        interpret=interpret,
    )(mine, other)


def swapped(bits):
    return [(i, i ^ bits) for i in range(PEERS)]


def along(xs, along_x):
    def moved(k):
        dy, dx = (0, k) if along_x else (k, 0)
        return [(SIDE * y + x, SIDE * ((y + dy) % SIDE) + (x + dx) % SIDE) for y in range(SIDE) for x in range(SIDE)]

    last, first, second = (lax.ppermute(xs[k - 1], "cols", moved(k)) for k in (2, 1, 3))
    return [first, last, second]


def on_device(values, tile_users, tile_items, tile_words, tile_count, factor_items, factor_words):
    across = swapped(1)
    around = [(2 * z, 2 * ((z + 1) % 8)) for z in range(8)] + [(2 * z + 1, 2 * ((z + 7) % 8) + 1) for z in range(8)]
    after = lax.optimization_barrier
    others = [lax.ppermute(x, "rows", across) for x in (factor_items, factor_words)]
    found = [jnp.concatenate([factor_items, factor_words, *others], axis=0)]
    highs, lows = [], []
    grams = partial_grams(found)
    more = lax.ppermute(grams, "cols", swapped(1))
    for step in range(4):
        arriving = lax.ppermute(found[-1] if step < 3 else found[-1][: 2 * ROWS], "rows", around)
        high, low = build_weights(values, tile_users, step, found[-1])
        if step == 0:
            grams = folded(found[-1], grams, more)
            arriving, low, grams = after((arriving, low, grams))
            more = lax.ppermute(grams, "cols", swapped(2))
        else:
            grams = folded(low if step == 1 else found[-1], grams, more)
            more = lax.ppermute(grams, *(("cols", swapped(2 << step)) if step < 3 else ("rows", swapped(2))))
            if step == 1:
                arriving, low = after((arriving, low))
            else:
                arriving, low, more = after((arriving, low, more))
        highs.append(high)
        lows.append(low)
        found.append(arriving)
    pieces = found + [lax.ppermute(x, "rows", across) for x in found[1:]]
    scalars = (tile_items, tile_words, tile_count)
    *out, own_a, parts = products(True, highs, lows, pieces=pieces, scalars=scalars)
    in_a = along(out, True)
    *out, own_b = products(False, highs, lows, parts=parts)
    in_b = along(out, False)
    grams = folded(own_b, grams, more)
    more = lax.ppermute(grams, "rows", swapped(4))
    own_a, more = after((own_a, more))
    *out, own_a = relayed(True, own_a, in_a)
    end_a = along(out, False)
    grams = folded(own_a, grams, more)
    more = lax.ppermute(grams, "rows", swapped(8))
    *out, own_b = relayed(False, own_b, in_b)
    end_b = along(out, True)
    grams = folded(own_b, grams, more, multiply=True)
    inverse = inverted(grams, lax.ppermute(grams, "rows", across))
    return finish((own_a, *end_a), (own_b, *end_b), inverse)


def solution(mesh):
    placed = (
        P(("rows", "cols"), None),
        P(("rows", "cols"), None),
        P(("rows", "cols")),
        P(("rows", "cols")),
        P(("rows", "cols")),
        P(("rows", "cols"), None),
        P(("rows", "cols"), None),
    )
    return jax.shard_map(
        on_device, mesh=mesh, in_specs=placed, out_specs=P(("rows", "cols"), None), check_vma=False
    )
```
